32 devices in a mesh: dp: 4 (over y, x), tensor: 8 (over z, core).
Axes of the slice: x: 2, y: 2, z: 4, core: 2. Of those that a mesh axis runs over, the one named last changes fastest.
Arguments:
- real_feats: bfloat16 [2048, 1536], P(('dp', 'tensor')), may hold values from -6 to 6
- fake_feats: bfloat16 [2048, 1536], P(('dp', 'tensor')), may hold values from -6 to 6
- mix_num: int32 [2048], P(('dp', 'tensor')), may hold values from 0 to 256
- w_first: bfloat16 [1536, 12288], P(None, 'tensor'), may hold values from -0.15625 to 0.15625
- bias: float32 [12288], P('tensor'), may hold values from -3 to 3
- head: float32 [12288], P('tensor'), may hold values from -0.0546875 to 0.0546875
Outputs:
- grad_w: float32 [1536, 12288], P('dp', 'tensor')
- grad_bias: float32 [12288], P('tensor')
- grad_head: float32 [12288], P('tensor')
- penalty: float32 [], replicated
The draws below stay inside these ranges and needn't reach their ends.
All inputs are finite; a program needn't handle non-finite values.
Results may differ from the reference program's by a relative error of at most 0.0005.
Values may be sent and summed in bfloat16 or wider, within the bound.
A program may use at most 64 MiB of HBM per device.

```python
import jax
import jax.numpy as jnp
from jax import lax

D = 1536
H = 12288
ROWS = 2048
BLOCK = 512


def plant(entries, rng, smallest, high):
    longest = entries.shape.index(max(entries.shape))
    spots = []
    for shift in (0, 1):
        where = [jax.random.randint(jax.random.fold_in(rng, axis), (), 0, length) for axis, length in enumerate(entries.shape)]
        where[longest] = (where[longest] + shift) % entries.shape[longest]
        spots.append(tuple(where))
    return entries.at[spots[0]].set(smallest).at[spots[1]].set(high)


def steps_of(own_key, extent, split, smallest, high):
    level, own = 1.0, jax.random.fold_in(own_key, 6)
    for axis_at, blocks in split:
        steps = jnp.exp(jax.random.uniform(jax.random.fold_in(own, axis_at), (blocks,), jnp.float32, smallest / len(split), high / len(split)))
        level = level * jnp.repeat(steps, extent[axis_at] // blocks).reshape([-1 if axis == axis_at else 1 for axis in range(len(extent))])
    return level


def centred(key, shape, deviation, bound, cuts=(), held_as=jnp.bfloat16):
    gain = steps_of(key, shape, cuts, -0.22, 0.18) if cuts else 1.0
    drawn = jax.random.normal(key, shape, jnp.float32) * deviation * gain
    return jnp.minimum(jnp.maximum(drawn, -bound), bound).astype(held_as)


def setup_inputs(seed: int = 0) -> dict:
    keys = jax.random.split(jax.random.key(seed), 7)
    real_feats = centred(keys[0], (ROWS, D), 1.0, 6.0, ((0, 32),))
    fake_feats = centred(keys[1], (ROWS, D), 1.0, 6.0, ((0, 32),))
    mix_num = plant(jax.random.randint(keys[2], (ROWS,), 0, 257), jax.random.fold_in(keys[2], 1), 0, 256).astype(jnp.int32)
    w_first = centred(keys[3], (D, H), D ** -0.5, 0.15625, ((1, 8),))
    bias = centred(keys[4], (H,), 0.5, 3.0, ((0, 8),), jnp.float32)
    head = centred(keys[5], (H,), H ** -0.5, 0.0546875, ((0, 8),), jnp.float32)
    return dict(real_feats=real_feats, fake_feats=fake_feats, mix_num=mix_num, w_first=w_first, bias=bias, head=head)


def block_terms(real_rows, fake_rows, mix_rows, w_first, bias, head):
    coef = mix_rows.astype(jnp.float32) / 256.0
    real_f = real_rows.astype(jnp.float32)
    mixed = (real_f + coef[:, None] * (fake_rows.astype(jnp.float32) - real_f)).astype(jnp.bfloat16)
    z = jnp.dot(mixed, w_first, preferred_element_type=jnp.float32) + bias
    sg = jax.nn.sigmoid(z)
    d1 = sg * (1.0 + z * (1.0 - sg))
    d2 = sg * (1.0 - sg) * (2.0 + z * (1.0 - 2.0 * sg))
    u = (d1 * head).astype(jnp.bfloat16)
    g = jnp.dot(u, w_first.T, preferred_element_type=jnp.float32)
    norm = jnp.sqrt(lax.optimization_barrier(jnp.sum(g * g, axis=1)) + 1e-06)
    scale = 20.0 * (norm - 1.0) / norm
    big = (scale[:, None] * g).astype(jnp.bfloat16)
    loss = jnp.sum((norm - 1.0) ** 2)
    p = jnp.dot(big, w_first, preferred_element_type=jnp.float32)
    dz = p * head * d2
    dzb = dz.astype(jnp.bfloat16)
    grad_w = jnp.dot(mixed.T, dzb, preferred_element_type=jnp.float32) + jnp.dot(big.T, u, preferred_element_type=jnp.float32)
    return (grad_w, lax.optimization_barrier(jnp.sum(dz, axis=0)), lax.optimization_barrier(jnp.sum(p * d1, axis=0)), loss)

def reference(real_feats, fake_feats, mix_num, w_first, bias, head):
    count = ROWS // BLOCK
    real_b = real_feats.reshape(count, BLOCK, D)
    fake_b = fake_feats.reshape(count, BLOCK, D)
    mix_b = mix_num.reshape(count, BLOCK)

    def step(carry, items):
        gw, gb, gh, total = block_terms(items[0], items[1], items[2], w_first, bias, head)
        return ((carry[0] + gw, carry[1] + gb, carry[2] + gh, carry[3] + total), None)
    init = (jnp.zeros((D, H), jnp.float32), jnp.zeros((H,), jnp.float32), jnp.zeros((H,), jnp.float32), jnp.zeros((), jnp.float32))
    sums, _ = lax.scan(step, init, (real_b, fake_b, mix_b))
    penalty = 10.0 * sums[3] / ROWS
    return (sums[0], sums[1], sums[2], penalty)
```

```python
import functools

import jax
import jax.numpy as jnp
from jax import lax
from jax.experimental import pallas as pl
from jax.experimental.pallas import tpu as pltpu
from jax.sharding import PartitionSpec as P

MESH = pl.DeviceIdType.MESH
VMEM_BYTES = 62 * 2**20
HELD_BYTES = 58 * 2**20


def row_contract(left, right):
    return lax.dot_general(
        left, right, (((0,), (0,)), ((), ())), preferred_element_type=jnp.float32
    )


def local(real_feats, fake_feats, mix_num, w_first, bias, head):
    coef = mix_num.astype(jnp.float32) / 256.0
    real_f = real_feats.astype(jnp.float32)
    mixed = (real_f + coef[:, None] * (fake_feats.astype(jnp.float32) - real_f)).astype(
        jnp.bfloat16
    )
    group = lax.all_gather(mixed, "tensor", axis=0, tiled=True)
    z = jnp.dot(group, w_first, preferred_element_type=jnp.float32) + bias
    sg = jax.nn.sigmoid(z)
    d1 = sg * (1.0 + z * (1.0 - sg))
    d2 = sg * (1.0 - sg) * (2.0 + z * (1.0 - 2.0 * sg))
    u = (d1 * head).astype(jnp.bfloat16)
    total_rows = group.shape[0] * lax.axis_size("dp")
    grad_in = lax.psum_scatter(
        lax.dot_general(
            u, w_first, (((1,), (1,)), ((), ())), preferred_element_type=jnp.float32
        ).astype(jnp.bfloat16),
        "tensor",
        scatter_dimension=0,
        tiled=True,
    ).astype(jnp.float32)
    norm = jnp.sqrt(jnp.sum(grad_in * grad_in, axis=1) + 1e-06)
    scale = 20.0 * (norm - 1.0) / norm
    scaled = (scale[:, None] * grad_in).astype(jnp.bfloat16)
    loss = lax.psum(jnp.sum((norm - 1.0) ** 2), ("dp", "tensor"))
    big = lax.all_gather(scaled, "tensor", axis=0, tiled=True)
    penalty = 10.0 * loss / total_rows
    p = jnp.dot(big, w_first, preferred_element_type=jnp.float32)
    dz = p * head * d2
    dzb = dz.astype(jnp.bfloat16)
    partial_w = row_contract(group, dzb)
    partial_w = partial_w + row_contract(big, u)
    grad_w = lax.psum_scatter(partial_w, "dp", scatter_dimension=0, tiled=True)
    grad_bias, grad_head = lax.psum((jnp.sum(dz, axis=0), jnp.sum(p * d1, axis=0)), "dp")
    return (grad_w, grad_bias, grad_head, penalty)


def flip(index, mask):
    bit = 1
    while bit <= mask:
        if mask & bit:
            index = index + bit - 2 * bit * lax.rem(index // bit, 2)
        bit *= 2
    return index


class Gather:
    def __init__(self, held, nz, send, recv, dev):
        self.held, self.nz, self.dev = held, nz, dev
        self.send, self.recv = send, recv
        self.names = (
            [("z", 0, k) for k in range(1, nz)]
            + [(kind, dx, k) for kind, dxs in (("c", range(4)), ("xy", (1, 2)), ("d", (0, 1)))
               for dx in dxs for k in range(nz)]
        )

    def copy(self, name):
        kind, dx, k = name
        held, dev = self.held, self.dev
        half = held.shape[3] // 2
        if kind == "z":
            src, dst, to = held.at[0, 0, 0], held.at[0, k, 0], dev(0, k, 0)
        elif kind == "c":
            src, dst, to = held.at[dx, k, 0], held.at[dx, k, 1], dev(0, 0, 1)
        elif kind == "xy":
            src, dst, to = held.at[0, k, 0], held.at[dx, k, 0], dev(dx, 0, 0)
        else:
            rows = pl.ds(dx * half, half)
            src, dst, to = held.at[1 + dx, k, 0, rows], held.at[3, k, 0, rows], dev(2 - dx, 0, 0)
        i = self.names.index(name)
        return pltpu.make_async_remote_copy(
            src_ref=src, dst_ref=dst, send_sem=self.send.at[i], recv_sem=self.recv.at[i],
            device_id=to, device_id_type=MESH,
        )

    def start(self):
        for k in range(1, self.nz):
            self.copy(("z", 0, k)).start()
        self.spread(0)

    def spread(self, k):
        if k:
            self.copy(("z", 0, k)).wait_recv()
        for name in (("xy", 1, k), ("xy", 2, k), ("c", 0, k)):
            self.copy(name).start()

    def turn(self, k):
        for dx in (1, 2):
            self.copy(("xy", dx, k)).wait_recv()
            self.copy(("d", dx - 1, k)).start()
            self.copy(("c", dx, k)).start()

    def last(self, k):
        self.copy(("d", 0, k)).wait_recv()
        self.copy(("d", 1, k)).wait_recv()
        self.copy(("c", 3, k)).start()

    def arrived(self, dx, ks):
        for k in ks:
            self.copy(("c", dx, k)).wait_recv()

    def finish(self):
        for name in self.names:
            self.copy(name).wait_send()


def kernel(
    nz, tile, total_rows,
    real, fake, mix, w_hbm, bias, head,
    out, out_bias, out_head, out_pen,
    w, mixed, big, u, d1, d2, own, lhs, to_pair, from_pair, to_z, from_z,
    sum_bias, sum_head, loss, loss_in,
    w_sem, m_send, m_recv, b_send, b_recv, p_send, p_recv, z_send, z_recv, l_send, l_recv,
):
    f32, bf16 = jnp.float32, jnp.bfloat16
    dp, tensor = lax.axis_index("dp"), lax.axis_index("tensor")
    z_at, core = tensor // 2, lax.rem(tensor, 2)
    rows, feats = real.shape
    hidden = w.shape[1]
    part = out.shape[0]
    pairs = nz // 2

    def dev(dx, zx, cc):
        return (flip(dp, dx), flip(z_at, zx) * 2 + flip(core, cc))

    load_w = pltpu.make_async_copy(w_hbm, w, w_sem)
    load_w.start()
    partners = [dev(0, 0, 1), dev(1, 0, 0), dev(2, 0, 0)]
    partners += [dev(0, k, 0) for k in range(1, nz)]
    barrier = pltpu.get_barrier_semaphore()
    for to in partners:
        pl.semaphore_signal(barrier, inc=1, device_id=to, device_id_type=MESH)
    coef = mix[...].astype(f32) / 256.0
    real_f = real[...].astype(f32)
    mixed[0, 0, 0] = (real_f + coef * (fake[...].astype(f32) - real_f)).astype(bf16)
    pl.semaphore_wait(barrier, len(partners))

    m_all = Gather(mixed, nz, m_send, m_recv, dev)
    b_all = Gather(big, nz, b_send, b_recv, dev)

    def block(held, dx, h):
        return held[dx, 2 * h:2 * h + 2].reshape(4 * rows, feats)

    def columns(i):
        return pl.ds(pl.multiple_of(i * tile, tile), tile)

    def hidden_units(dx, h):
        m_all.arrived(dx, (2 * h, 2 * h + 1))

        def step(i, carry):
            cols = columns(i)
            z = jnp.dot(block(mixed, dx, h), w[:, cols], preferred_element_type=f32)
            z = z + bias[:, cols]
            t = jnp.tanh(0.5 * z)
            sg = 0.5 + 0.5 * t
            slope = 0.25 * (1.0 - t * t)
            first = sg + z * slope
            second = slope * (2.0 - z * t)
            head_row = head[:, cols]
            d1[dx, h, :, cols] = first
            d2[dx, h, :, cols] = second * head_row
            u[dx, h, :, cols] = (first * head_row).astype(bf16)
            return carry

        lax.fori_loop(0, hidden // tile, step, 0)

    def pair_copy(k):
        return pltpu.make_async_remote_copy(
            src_ref=to_pair.at[k], dst_ref=from_pair.at[k], send_sem=p_send.at[k],
            recv_sem=p_recv.at[k], device_id=dev(0, 0, 1), device_id_type=MESH,
        )

    def z_copy(k):
        return pltpu.make_async_remote_copy(
            src_ref=to_z.at[k], dst_ref=from_z.at[k], send_sem=z_send.at[k],
            recv_sem=z_recv.at[k], device_id=dev(0, k, 0), device_id_type=MESH,
        )

    def input_gradient(h):
        def step(i, carry):
            cols = columns(i)
            g = lax.dot_general(
                u[0, h], w[cols, :], (((1,), (1,)), ((), ())), preferred_element_type=f32
            ).reshape(2, 2, rows, tile)
            for j in range(2):
                own[2 * h + j, :, cols] = g[j, 0]
                to_pair[2 * h + j, :, cols] = g[j, 1].astype(bf16)
            return carry

        lax.fori_loop(0, feats // tile, step, 0)
        for j in range(2):
            pair_copy(2 * h + j).start()

    def pair_sum(k):
        pair_copy(k).wait_recv()
        both = own[k] + from_pair[k].astype(f32)
        if k:
            to_z[k] = both.astype(bf16)
            z_copy(k).start()
        else:
            own[0] = both

    def weight_terms(dx, h, start):
        b_all.arrived(dx, (2 * h, 2 * h + 1))
        mine = pl.ds(pl.multiple_of(dp * part, 128), part)
        for j, held in enumerate((mixed, big)):
            lhs[j] = held[dx, 2 * h:2 * h + 2, :, :, mine].reshape(4 * rows, part).T

        def step(i, carry):
            cols = columns(i)
            p = jnp.dot(block(big, dx, h), w[:, cols], preferred_element_type=f32)
            dz = p * d2[dx, h, :, cols]
            ph = p * d1[dx, h, :, cols]
            add_bias = jnp.sum(dz.reshape(4 * rows // 8, 8, tile), axis=0)
            add_head = jnp.sum(ph.reshape(4 * rows // 8, 8, tile), axis=0)
            if h == 0:
                sum_bias[dx, :, cols] = add_bias
                sum_head[dx, :, cols] = add_head
            else:
                sum_bias[dx, :, cols] += add_bias
                sum_head[dx, :, cols] += add_head
            term = jnp.dot(lhs[0], dz.astype(bf16), preferred_element_type=f32)
            term = term + jnp.dot(lhs[1], u[dx, h, :, cols], preferred_element_type=f32)
            if start:
                out[:, cols] = term
            else:
                out[:, cols] += term
            return carry

        lax.fori_loop(0, hidden // tile, step, 0)

    def loss_copy(i, to):
        return pltpu.make_async_remote_copy(
            src_ref=loss.at[i], dst_ref=loss_in.at[i], send_sem=l_send.at[i],
            recv_sem=l_recv.at[i], device_id=to, device_id_type=MESH,
        )

    m_all.start()
    load_w.wait()
    for h in range(pairs):
        for k in (2 * h, 2 * h + 1):
            if k:
                m_all.spread(k)
        hidden_units(0, h)
        input_gradient(h)
        if h:
            for k in (2 * h - 2, 2 * h - 1):
                pair_sum(k)
    for k in (nz - 2, nz - 1):
        pair_sum(k)

    for h in range(pairs):
        for k in (2 * h, 2 * h + 1):
            m_all.turn(k)
        hidden_units(1, h)
    for h in range(pairs):
        hidden_units(2, h)

    g = own[0]
    for k in range(1, nz):
        z_copy(k).wait_recv()
        g = g + from_z[k].astype(f32)
    norm = jnp.sqrt(jnp.sum(g * g, axis=1, keepdims=True) + 1e-06)
    big[0, 0, 0] = (20.0 * (norm - 1.0) / norm * g).astype(bf16)
    b_all.start()
    miss = jnp.sum((norm - 1.0) ** 2, axis=0, keepdims=True)
    loss[0] = jnp.broadcast_to(miss, loss.shape[1:])

    hops = [dev(0, 0, 1)]
    bit = 1
    while bit < nz:
        hops.append(dev(0, bit, 0))
        bit *= 2
    hops += [dev(1, 0, 0), dev(2, 0, 0)]
    loss_copy(0, hops[0]).start()
    state = [0]

    def loss_step():
        i = state[0]
        if i < len(hops):
            loss_copy(i, hops[i]).wait_recv()
            loss[i + 1] = loss[i] + loss_in[i]
            if i + 1 < len(hops):
                loss_copy(i + 1, hops[i + 1]).start()
            state[0] = i + 1

    for k in range(nz):
        m_all.last(k)
    for h in range(pairs):
        for k in (2 * h, 2 * h + 1):
            if k:
                b_all.spread(k)
        hidden_units(3, h)
        loss_step()

    order = []
    for h in range(pairs):
        order.append((0, h))
    for h in range(pairs):
        order.append((1, h))
        order.append((2, h))
    for h in range(pairs):
        order.append((3, h))
    turned, ended = 0, 0
    for n, (dx, h) in enumerate(order):
        while turned < nz and (turned <= n or (dx and turned < 2 * h + 2)):
            b_all.turn(turned)
            turned += 1
        while ended < nz and (dx == 3 and ended < 2 * h + 2 or ended + nz <= n):
            b_all.last(ended)
            ended += 1
        weight_terms(dx, h, n == 0)
        loss_step()
    while state[0] < len(hops):
        loss_step()

    for ref, sums in ((out_bias, sum_bias), (out_head, sum_head)):
        whole = (sums[0] + sums[1]) + (sums[2] + sums[3])
        ref[...] = jnp.sum(whole, axis=0, keepdims=True)
    out_pen[...] = 10.0 * loss[len(hops)] / total_rows

    m_all.finish()
    b_all.finish()
    for k in range(nz):
        pair_copy(k).wait_send()
        if k:
            z_copy(k).wait_send()
    for i, to in enumerate(hops):
        loss_copy(i, to).wait_send()


def scratch_of(rows, feats, hidden, part, nz):
    f32, bf16 = jnp.float32, jnp.bfloat16
    hops = nz.bit_length() + 2
    held = [
        ((feats, hidden), bf16),
        ((4, nz, 2, rows, feats), bf16),
        ((4, nz, 2, rows, feats), bf16),
        ((4, nz // 2, 4 * rows, hidden), bf16),
        ((4, nz // 2, 4 * rows, hidden), f32),
        ((4, nz // 2, 4 * rows, hidden), f32),
        ((nz, rows, feats), f32),
        ((2, part, 4 * rows), bf16),
        ((nz, rows, feats), bf16),
        ((nz, rows, feats), bf16),
        ((nz, rows, feats), bf16),
        ((nz, rows, feats), bf16),
        ((4, 8, hidden), f32),
        ((4, 8, hidden), f32),
        ((hops + 1, 8, 128), f32),
        ((hops + 1, 8, 128), f32),
    ]
    moves = nz - 1 + 8 * nz
    sems = [(), (moves,), (moves,), (moves,), (moves,), (nz,), (nz,), (nz,), (nz,), (hops,), (hops,)]
    return held, sems


def solution(mesh):
    placed = (
        P(("dp", "tensor"), None),
        P(("dp", "tensor"), None),
        P(("dp", "tensor")),
        P(None, "tensor"),
        P("tensor"),
        P("tensor"),
    )
    groups, members = mesh.shape["dp"], mesh.shape["tensor"]
    nz = members // 2

    def body(real_feats, fake_feats, mix_num, w_first, bias, head):
        rows, feats = real_feats.shape
        hidden = w_first.shape[1]
        part = feats // groups
        held, sems = scratch_of(rows, feats, hidden, part, max(nz, 2))
        size = part * hidden * 4
        for shape, dtype in held:
            size += functools.reduce(lambda a, b: a * b, shape) * jnp.dtype(dtype).itemsize
        tile = next((t for t in (512, 256, 128) if hidden % t == 0 and feats % t == 0), 0)
        fits = (
            groups == 4 and members % 2 == 0 and nz >= 2 and nz & (nz - 1) == 0
            and tile and rows % 32 == 0 and part % 128 == 0 and size <= HELD_BYTES
        )
        if not fits:
            return local(real_feats, fake_feats, mix_num, w_first, bias, head)
        vmem = pl.BlockSpec(memory_space=pltpu.VMEM)
        total_rows = rows * groups * members
        grad_w, grad_bias, grad_head, pen = pl.pallas_call(
            functools.partial(kernel, nz, tile, total_rows),
            out_shape=(
                jax.ShapeDtypeStruct((part, hidden), jnp.float32),
                jax.ShapeDtypeStruct((1, hidden), jnp.float32),
                jax.ShapeDtypeStruct((1, hidden), jnp.float32),
                jax.ShapeDtypeStruct((8, 128), jnp.float32),
            ),
            in_specs=[vmem, vmem, vmem, pl.BlockSpec(memory_space=pl.ANY), vmem, vmem],
            out_specs=(vmem, vmem, vmem, vmem),
            scratch_shapes=[pltpu.VMEM(s, t) for s, t in held]
            + [pltpu.SemaphoreType.DMA(s) if s else pltpu.SemaphoreType.DMA for s in sems],
            compiler_params=pltpu.CompilerParams(
                collective_id=0, has_side_effects=True, vmem_limit_bytes=VMEM_BYTES
            ),
        )(real_feats, fake_feats, mix_num[:, None], w_first, bias[None], head[None])
        return (grad_w, grad_bias[0], grad_head[0], pen[0, 0])

    return jax.shard_map(
        body,
        mesh=mesh,
        in_specs=placed,
        out_specs=(P("dp", "tensor"), P("tensor"), P("tensor"), P()),
        check_vma=False,
    )
```

```python
import functools

import jax
import jax.numpy as jnp
from jax import lax
from jax.experimental import pallas as pl
from jax.experimental.pallas import tpu as pltpu
from jax.sharding import PartitionSpec as P

MESH = pl.DeviceIdType.MESH
VMEM_BYTES = 62 * 2**20
HELD_BYTES = 58 * 2**20


def row_contract(left, right):
    return lax.dot_general(
        left, right, (((0,), (0,)), ((), ())), preferred_element_type=jnp.float32
    )


def local(real_feats, fake_feats, mix_num, w_first, bias, head):
    coef = mix_num.astype(jnp.float32) / 256.0
    real_f = real_feats.astype(jnp.float32)
    mixed = (real_f + coef[:, None] * (fake_feats.astype(jnp.float32) - real_f)).astype(
        jnp.bfloat16
    )
    group = lax.all_gather(mixed, "tensor", axis=0, tiled=True)
    z = jnp.dot(group, w_first, preferred_element_type=jnp.float32) + bias
    sg = jax.nn.sigmoid(z)
    d1 = sg * (1.0 + z * (1.0 - sg))
    d2 = sg * (1.0 - sg) * (2.0 + z * (1.0 - 2.0 * sg))
    u = (d1 * head).astype(jnp.bfloat16)
    total_rows = group.shape[0] * lax.axis_size("dp")
    grad_in = lax.psum_scatter(
        lax.dot_general(
            u, w_first, (((1,), (1,)), ((), ())), preferred_element_type=jnp.float32
        ).astype(jnp.bfloat16),
        "tensor",
        scatter_dimension=0,
        tiled=True,
    ).astype(jnp.float32)
    norm = jnp.sqrt(jnp.sum(grad_in * grad_in, axis=1) + 1e-06)
    scale = 20.0 * (norm - 1.0) / norm
    scaled = (scale[:, None] * grad_in).astype(jnp.bfloat16)
    loss = lax.psum(jnp.sum((norm - 1.0) ** 2), ("dp", "tensor"))
    big = lax.all_gather(scaled, "tensor", axis=0, tiled=True)
    penalty = 10.0 * loss / total_rows
    p = jnp.dot(big, w_first, preferred_element_type=jnp.float32)
    dz = p * head * d2
    dzb = dz.astype(jnp.bfloat16)
    partial_w = row_contract(group, dzb)
    partial_w = partial_w + row_contract(big, u)
    grad_w = lax.psum_scatter(partial_w, "dp", scatter_dimension=0, tiled=True)
    grad_bias, grad_head = lax.psum((jnp.sum(dz, axis=0), jnp.sum(p * d1, axis=0)), "dp")
    return (grad_w, grad_bias, grad_head, penalty)


def flip(index, mask):
    bit = 1
    while bit <= mask:
        if mask & bit:
            index = index + bit - 2 * bit * lax.rem(index // bit, 2)
        bit *= 2
    return index


class Gather:
    def __init__(self, held, nz, send, recv, dev):
        self.held, self.nz, self.dev = held, nz, dev
        self.send, self.recv = send, recv
        self.names = (
            [("z", 0, k) for k in range(1, nz)]
            + [(kind, dx, k) for kind, dxs in (("c", range(4)), ("xy", (1, 2)), ("d", (0, 1)))
               for dx in dxs for k in range(nz)]
        )

    def copy(self, name):
        kind, dx, k = name
        held, dev = self.held, self.dev
        half = held.shape[3] // 2
        if kind == "z":
            src, dst, to = held.at[0, 0, 0], held.at[0, k, 0], dev(0, k, 0)
        elif kind == "c":
            src, dst, to = held.at[dx, k, 0], held.at[dx, k, 1], dev(0, 0, 1)
        elif kind == "xy":
            src, dst, to = held.at[0, k, 0], held.at[dx, k, 0], dev(dx, 0, 0)
        else:
            rows = pl.ds(dx * half, half)
            src, dst, to = held.at[1 + dx, k, 0, rows], held.at[3, k, 0, rows], dev(2 - dx, 0, 0)
        i = self.names.index(name)
        return pltpu.make_async_remote_copy(
            src_ref=src, dst_ref=dst, send_sem=self.send.at[i], recv_sem=self.recv.at[i],
            device_id=to, device_id_type=MESH,
        )

    def start(self):
        for k in range(1, self.nz):
            self.copy(("z", 0, k)).start()
        self.spread(0)

    def spread(self, *ks):
        for k in ks:
            if k:
                self.copy(("z", 0, k)).wait_recv()
            for name in (("xy", 1, k), ("xy", 2, k), ("c", 0, k)):
                self.copy(name).start()

    def turn(self, *ks):
        for k in ks:
            for dx in (1, 2):
                self.copy(("xy", dx, k)).wait_recv()
                self.copy(("d", dx - 1, k)).start()
                self.copy(("c", dx, k)).start()

    def last(self, *ks):
        for k in ks:
            self.copy(("d", 0, k)).wait_recv()
            self.copy(("d", 1, k)).wait_recv()
            self.copy(("c", 3, k)).start()

    def arrived(self, dx):
        for k in range(self.nz):
            self.copy(("c", dx, k)).wait_recv()

    def finish(self):
        for name in self.names:
            self.copy(name).wait_send()


def kernel(
    nz, tile, total_rows,
    real, fake, mix, w_hbm, bias, head,
    out, out_bias, out_head, out_pen,
    w, mixed, big, u, d1, d2, own, lhs, to_pair, from_pair, to_z, from_z,
    sum_bias, sum_head, loss, loss_in, bias_row, head_row,
    w_sem, m_send, m_recv, b_send, b_recv, p_send, p_recv, z_send, z_recv, l_send, l_recv,
):
    f32, bf16 = jnp.float32, jnp.bfloat16
    dp, tensor = lax.axis_index("dp"), lax.axis_index("tensor")
    z_at, core = tensor // 2, lax.rem(tensor, 2)
    feats = real.shape[1]
    rows = real.shape[0] // 2
    lot = 2 * nz * rows
    hidden = w.shape[1]
    part = out.shape[0]
    every, others = tuple(range(nz)), tuple(range(1, nz))

    def dev(dx, zx, cc):
        return (flip(dp, dx), flip(z_at, zx) * 2 + flip(core, cc))

    load_w = pltpu.make_async_copy(w_hbm, w, w_sem)
    load_w.start()
    partners = [dev(0, 0, 1), dev(1, 0, 0), dev(2, 0, 0)]
    partners += [dev(0, k, 0) for k in others]
    barrier = pltpu.get_barrier_semaphore()
    for to in partners:
        pl.semaphore_signal(barrier, inc=1, device_id=to, device_id_type=MESH)
    count = mix.shape[0]
    places = [lax.broadcasted_iota(jnp.int32, (count, count), axis) for axis in (0, 1)]
    spread = jnp.broadcast_to(mix[...].reshape(1, count).astype(f32), (count, count))
    spread = jnp.where(places[0] == places[1], spread, 0.0)
    coef = jnp.sum(spread, axis=1, keepdims=True) / 256.0
    real_f = real[...].astype(f32)
    rows_in = (real_f + coef * (fake[...].astype(f32) - real_f)).astype(bf16)
    for h in range(2):
        mixed[h, 0, 0, 0] = rows_in[h * rows:(h + 1) * rows]
    bias_row[...] = bias[...].reshape(1, hidden)
    head_row[...] = head[...].reshape(1, hidden)
    pl.semaphore_wait(barrier, len(partners))

    m_all = [Gather(mixed.at[h], nz, m_send.at[h], m_recv.at[h], dev) for h in range(2)]
    b_all = [Gather(big.at[h], nz, b_send.at[h], b_recv.at[h], dev) for h in range(2)]

    def block(held, dx, h):
        return held[h, dx].reshape(lot, feats)

    def columns(i):
        return pl.ds(pl.multiple_of(i * tile, tile), tile)

    def hidden_units(dx, h):
        m_all[h].arrived(dx)

        def step(i, carry):
            cols = columns(i)
            z = jnp.dot(block(mixed, dx, h), w[:, cols], preferred_element_type=f32)
            z = z + bias_row[:, cols]
            t = jnp.tanh(0.5 * z)
            sg = 0.5 + 0.5 * t
            slope = 0.25 * (1.0 - t * t)
            first = sg + z * slope
            second = slope * (2.0 - z * t)
            by = head_row[:, cols]
            d1[dx, h, :, cols] = first
            d2[dx, h, :, cols] = second * by
            u[dx, h, :, cols] = (first * by).astype(bf16)
            return carry

        lax.fori_loop(0, hidden // tile, step, 0)

    def pair_copy(h):
        return pltpu.make_async_remote_copy(
            src_ref=to_pair.at[h], dst_ref=from_pair.at[h], send_sem=p_send.at[h],
            recv_sem=p_recv.at[h], device_id=dev(0, 0, 1), device_id_type=MESH,
        )

    def z_copy(h, k):
        return pltpu.make_async_remote_copy(
            src_ref=to_z.at[h, k], dst_ref=from_z.at[h, k], send_sem=z_send.at[h, k],
            recv_sem=z_recv.at[h, k], device_id=dev(0, k, 0), device_id_type=MESH,
        )

    def input_gradient(h):
        def step(i, carry):
            cols = columns(i)
            g = lax.dot_general(
                u[0, h], w[cols, :], (((1,), (1,)), ((), ())), preferred_element_type=f32
            ).reshape(nz, 2, rows, tile)
            for k in every:
                own[h, k, :, cols] = g[k, 0]
                to_pair[h, k, :, cols] = g[k, 1].astype(bf16)
            return carry

        lax.fori_loop(0, feats // tile, step, 0)
        pair_copy(h).start()

    def pair_sum(h):
        pair_copy(h).wait_recv()
        for k in others + (0,):
            both = own[h, k] + from_pair[h, k].astype(f32)
            if k:
                to_z[h, k] = both.astype(bf16)
                z_copy(h, k).start()
            else:
                own[h, 0] = both

    def scale_rows(h):
        g = own[h, 0]
        for k in others:
            z_copy(h, k).wait_recv()
            g = g + from_z[h, k].astype(f32)
        norm = jnp.sqrt(jnp.sum(g * g, axis=1, keepdims=True) + 1e-06)
        big[h, 0, 0, 0] = (20.0 * (norm - 1.0) / norm * g).astype(bf16)
        b_all[h].start()
        return jnp.sum((norm - 1.0) ** 2, axis=0, keepdims=True)

    def weight_terms(dx, h, start=False):
        b_all[h].arrived(dx)
        mine = pl.ds(pl.multiple_of(dp * part, 128), part)
        for j, held in enumerate((mixed, big)):
            lhs[j] = held[h, dx, :, :, :, mine].reshape(lot, part).T

        def step(i, carry):
            cols = columns(i)
            p = jnp.dot(block(big, dx, h), w[:, cols], preferred_element_type=f32)
            dz = p * d2[dx, h, :, cols]
            ph = p * d1[dx, h, :, cols]
            add_bias = jnp.sum(dz.reshape(lot // 8, 8, tile), axis=0)
            add_head = jnp.sum(ph.reshape(lot // 8, 8, tile), axis=0)
            if h == 0:
                sum_bias[dx, :, cols] = add_bias
                sum_head[dx, :, cols] = add_head
            else:
                sum_bias[dx, :, cols] += add_bias
                sum_head[dx, :, cols] += add_head
            term = jnp.dot(lhs[0], dz.astype(bf16), preferred_element_type=f32)
            term = term + jnp.dot(lhs[1], u[dx, h, :, cols], preferred_element_type=f32)
            if start:
                out[:, cols] = term
            else:
                out[:, cols] += term
            return carry

        lax.fori_loop(0, hidden // tile, step, 0)

    hops = [dev(0, 0, 1)]
    bit = 1
    while bit < nz:
        hops.append(dev(0, bit, 0))
        bit *= 2
    hops += [dev(1, 0, 0), dev(2, 0, 0)]

    def loss_copy(i):
        return pltpu.make_async_remote_copy(
            src_ref=loss.at[i], dst_ref=loss_in.at[i], send_sem=l_send.at[i],
            recv_sem=l_recv.at[i], device_id=hops[i], device_id_type=MESH,
        )

    state = [0]

    def loss_step():
        i = state[0]
        if i < len(hops):
            loss_copy(i).wait_recv()
            loss[i + 1] = loss[i] + loss_in[i]
            if i + 1 < len(hops):
                loss_copy(i + 1).start()
            state[0] = i + 1

    m_all[0].start()
    m_all[1].start()
    load_w.wait()
    m_all[0].spread(*others)
    hidden_units(0, 0)
    input_gradient(0)
    m_all[0].turn(*every)
    hidden_units(1, 0)
    pair_sum(0)
    m_all[1].spread(*others)
    hidden_units(0, 1)
    input_gradient(1)
    m_all[0].last(*every)
    hidden_units(2, 0)
    pair_sum(1)
    miss = scale_rows(0)
    hidden_units(3, 0)
    b_all[0].spread(1)
    m_all[1].turn(*every)
    hidden_units(1, 1)
    b_all[0].spread(*others[1:])
    hidden_units(2, 1)
    miss = miss + scale_rows(1)
    loss[0] = jnp.broadcast_to(miss, loss.shape[1:])
    loss_copy(0).start()
    m_all[1].last(*every)
    b_all[0].turn(0, 1)
    hidden_units(3, 1)
    loss_step()

    b_all[0].turn(*every[2:])
    b_all[1].spread(1)
    weight_terms(0, 0, True)
    loss_step()
    b_all[1].spread(*others[1:])
    weight_terms(1, 0)
    loss_step()
    b_all[0].last(*every)
    b_all[1].turn(0, 1)
    weight_terms(2, 0)
    loss_step()
    b_all[1].turn(*every[2:])
    weight_terms(3, 0)
    loss_step()
    weight_terms(0, 1)
    b_all[1].last(*every)
    weight_terms(1, 1)
    weight_terms(2, 1)
    weight_terms(3, 1)
    while state[0] < len(hops):
        loss_step()

    for ref, sums in ((out_bias, sum_bias), (out_head, sum_head)):
        whole = (sums[0] + sums[1]) + (sums[2] + sums[3])
        ref[...] = jnp.sum(whole, axis=0, keepdims=True).reshape(hidden)
    out_pen[0, 0] = (10.0 * loss[len(hops)] / total_rows)[0, 0]

    for h in range(2):
        m_all[h].finish()
        b_all[h].finish()
        pair_copy(h).wait_send()
        for k in others:
            z_copy(h, k).wait_send()
    for i in range(len(hops)):
        loss_copy(i).wait_send()


def scratch_of(rows, feats, hidden, part, nz):
    f32, bf16 = jnp.float32, jnp.bfloat16
    hops = nz.bit_length() + 2
    lot = nz * rows
    held = [
        ((feats, hidden), bf16),
        ((2, 4, nz, 2, rows // 2, feats), bf16),
        ((2, 4, nz, 2, rows // 2, feats), bf16),
        ((4, 2, lot, hidden), bf16),
        ((4, 2, lot, hidden), f32),
        ((4, 2, lot, hidden), f32),
        ((2, nz, rows // 2, feats), f32),
        ((2, part, lot), bf16),
        ((2, nz, rows // 2, feats), bf16),
        ((2, nz, rows // 2, feats), bf16),
        ((2, nz, rows // 2, feats), bf16),
        ((2, nz, rows // 2, feats), bf16),
        ((4, 8, hidden), f32),
        ((4, 8, hidden), f32),
        ((hops + 1, 8, 128), f32),
        ((hops + 1, 8, 128), f32),
        ((1, hidden), f32),
        ((1, hidden), f32),
    ]
    moves = nz - 1 + 8 * nz
    sems = [(), (2, moves), (2, moves), (2, moves), (2, moves), (2,), (2,), (2, nz), (2, nz), (hops,), (hops,)]
    return held, sems


def solution(mesh):
    placed = (
        P(("dp", "tensor"), None),
        P(("dp", "tensor"), None),
        P(("dp", "tensor")),
        P(None, "tensor"),
        P("tensor"),
        P("tensor"),
    )
    groups, members = mesh.shape["dp"], mesh.shape["tensor"]
    nz = members // 2

    def body(real_feats, fake_feats, mix_num, w_first, bias, head):
        rows, feats = real_feats.shape
        hidden = w_first.shape[1]
        part = feats // groups
        held, sems = scratch_of(rows, feats, hidden, part, max(nz, 2))
        size = part * hidden * 4
        for shape, dtype in held:
            size += functools.reduce(lambda a, b: a * b, shape) * jnp.dtype(dtype).itemsize
        tile = next((t for t in (512, 256, 128) if hidden % t == 0 and feats % t == 0), 0)
        fits = (
            groups == 4 and members % 2 == 0 and nz >= 2 and nz & (nz - 1) == 0
            and tile and rows % 64 == 0 and part % 128 == 0 and size <= HELD_BYTES
        )
        if not fits:
            return local(real_feats, fake_feats, mix_num, w_first, bias, head)
        vmem = pl.BlockSpec(memory_space=pltpu.VMEM)
        total_rows = rows * groups * members
        grad_w, grad_bias, grad_head, pen = pl.pallas_call(
            functools.partial(kernel, nz, tile, total_rows),
            out_shape=(
                jax.ShapeDtypeStruct((part, hidden), jnp.float32),
                jax.ShapeDtypeStruct((hidden,), jnp.float32),
                jax.ShapeDtypeStruct((hidden,), jnp.float32),
                jax.ShapeDtypeStruct((1, 1), jnp.float32),
            ),
            in_specs=[vmem, vmem, vmem, pl.BlockSpec(memory_space=pl.ANY), vmem, vmem],
            out_specs=(vmem, vmem, vmem, pl.BlockSpec(memory_space=pltpu.SMEM)),
            scratch_shapes=[pltpu.VMEM(s, t) for s, t in held]
            + [pltpu.SemaphoreType.DMA(s) if s else pltpu.SemaphoreType.DMA for s in sems],
            compiler_params=pltpu.CompilerParams(
                collective_id=0, has_side_effects=True, vmem_limit_bytes=VMEM_BYTES
            ),
        )(real_feats, fake_feats, mix_num, w_first, bias, head)
        return (grad_w, grad_bias, grad_head, pen.reshape(()))

    return jax.shard_map(
        body,
        mesh=mesh,
        in_specs=placed,
        out_specs=(P("dp", "tensor"), P("tensor"), P("tensor"), P()),
        check_vma=False,
    )
```

```python
import functools

import jax
import jax.numpy as jnp
from jax import lax
from jax.experimental import pallas as pl
from jax.experimental.pallas import tpu as pltpu
from jax.sharding import PartitionSpec as P

MESH = pl.DeviceIdType.MESH
VMEM_BYTES = 62 * 2**20
HELD_BYTES = 58 * 2**20


def row_contract(left, right):
    return lax.dot_general(
        left, right, (((0,), (0,)), ((), ())), preferred_element_type=jnp.float32
    )


def local(real_feats, fake_feats, mix_num, w_first, bias, head):
    coef = mix_num.astype(jnp.float32) / 256.0
    real_f = real_feats.astype(jnp.float32)
    mixed = (real_f + coef[:, None] * (fake_feats.astype(jnp.float32) - real_f)).astype(
        jnp.bfloat16
    )
    group = lax.all_gather(mixed, "tensor", axis=0, tiled=True)
    z = jnp.dot(group, w_first, preferred_element_type=jnp.float32) + bias
    sg = jax.nn.sigmoid(z)
    d1 = sg * (1.0 + z * (1.0 - sg))
    d2 = sg * (1.0 - sg) * (2.0 + z * (1.0 - 2.0 * sg))
    u = (d1 * head).astype(jnp.bfloat16)
    total_rows = group.shape[0] * lax.axis_size("dp")
    grad_in = lax.psum_scatter(
        lax.dot_general(
            u, w_first, (((1,), (1,)), ((), ())), preferred_element_type=jnp.float32
        ).astype(jnp.bfloat16),
        "tensor",
        scatter_dimension=0,
        tiled=True,
    ).astype(jnp.float32)
    norm = jnp.sqrt(jnp.sum(grad_in * grad_in, axis=1) + 1e-06)
    scale = 20.0 * (norm - 1.0) / norm
    scaled = (scale[:, None] * grad_in).astype(jnp.bfloat16)
    loss = lax.psum(jnp.sum((norm - 1.0) ** 2), ("dp", "tensor"))
    big = lax.all_gather(scaled, "tensor", axis=0, tiled=True)
    penalty = 10.0 * loss / total_rows
    p = jnp.dot(big, w_first, preferred_element_type=jnp.float32)
    dz = p * head * d2
    dzb = dz.astype(jnp.bfloat16)
    partial_w = row_contract(group, dzb)
    partial_w = partial_w + row_contract(big, u)
    grad_w = lax.psum_scatter(partial_w, "dp", scatter_dimension=0, tiled=True)
    grad_bias, grad_head = lax.psum((jnp.sum(dz, axis=0), jnp.sum(p * d1, axis=0)), "dp")
    return (grad_w, grad_bias, grad_head, penalty)


def flip(index, mask):
    bit = 1
    while bit <= mask:
        if mask & bit:
            index = index + bit - 2 * bit * lax.rem(index // bit, 2)
        bit *= 2
    return index


class Gather:
    def __init__(self, held, nz, send, recv, dev):
        self.held, self.nz, self.dev = held, nz, dev
        self.send, self.recv = send, recv
        self.names = (
            [("z", 0, k) for k in range(1, nz)]
            + [(kind, dx, k) for kind, dxs in (("c", range(4)), ("xy", (1, 2)), ("d", (0, 1)))
               for dx in dxs for k in range(nz)]
        )

    def copy(self, name):
        kind, dx, k = name
        held, dev = self.held, self.dev
        half = held.shape[3] // 2
        if kind == "z":
            src, dst, to = held.at[0, 0, 0], held.at[0, k, 0], dev(0, k, 0)
        elif kind == "c":
            src, dst, to = held.at[dx, k, 0], held.at[dx, k, 1], dev(0, 0, 1)
        elif kind == "xy":
            src, dst, to = held.at[0, k, 0], held.at[dx, k, 0], dev(dx, 0, 0)
        else:
            rows = pl.ds(dx * half, half)
            src, dst, to = held.at[1 + dx, k, 0, rows], held.at[3, k, 0, rows], dev(2 - dx, 0, 0)
        i = self.names.index(name)
        return pltpu.make_async_remote_copy(
            src_ref=src, dst_ref=dst, send_sem=self.send.at[i], recv_sem=self.recv.at[i],
            device_id=to, device_id_type=MESH,
        )

    def start(self):
        for k in range(1, self.nz):
            self.copy(("z", 0, k)).start()
        self.spread(0)

    def spread(self, *ks):
        for k in ks:
            if k:
                self.copy(("z", 0, k)).wait_recv()
            for name in (("xy", 1, k), ("xy", 2, k), ("c", 0, k)):
                self.copy(name).start()

    def turn(self, *ks):
        for k in ks:
            for dx in (1, 2):
                self.copy(("xy", dx, k)).wait_recv()
                self.copy(("d", dx - 1, k)).start()
                self.copy(("c", dx, k)).start()

    def last(self, *ks):
        for k in ks:
            self.copy(("d", 0, k)).wait_recv()
            self.copy(("d", 1, k)).wait_recv()
            self.copy(("c", 3, k)).start()

    def finish(self):
        for name in self.names:
            self.copy(name).wait_send()


def kernel(
    nz, tile, total_rows,
    real, fake, mix, w_hbm, bias, head,
    out, out_bias, out_head, out_pen,
    w, mixed, big, u, d1, d2, own, lhs, to_pair, from_pair, to_z, from_z,
    sum_bias, sum_head, loss, loss_in, bias_row, head_row,
    w_sem, m_send, m_recv, b_send, b_recv, p_send, p_recv, z_send, z_recv, l_send, l_recv,
):
    f32, bf16 = jnp.float32, jnp.bfloat16
    dp, tensor = lax.axis_index("dp"), lax.axis_index("tensor")
    z_at, core = tensor // 2, lax.rem(tensor, 2)
    feats = real.shape[1]
    rows = real.shape[0] // 2
    lot = 2 * nz * rows
    hidden = w.shape[1]
    part = out.shape[0]
    every, others = tuple(range(nz)), tuple(range(1, nz))

    def dev(dx, zx, cc):
        return (flip(dp, dx), flip(z_at, zx) * 2 + flip(core, cc))

    load_w = pltpu.make_async_copy(w_hbm, w, w_sem)
    load_w.start()
    partners = [dev(0, 0, 1), dev(1, 0, 0), dev(2, 0, 0)]
    partners += [dev(0, k, 0) for k in others]
    barrier = pltpu.get_barrier_semaphore()
    for to in partners:
        pl.semaphore_signal(barrier, inc=1, device_id=to, device_id_type=MESH)
    count = mix.shape[0]
    places = [lax.broadcasted_iota(jnp.int32, (count, count), axis) for axis in (0, 1)]
    spread = jnp.broadcast_to(mix[...].reshape(1, count).astype(f32), (count, count))
    spread = jnp.where(places[0] == places[1], spread, 0.0)
    coef = jnp.sum(spread, axis=1, keepdims=True) / 256.0
    real_f = real[...].astype(f32)
    rows_in = (real_f + coef * (fake[...].astype(f32) - real_f)).astype(bf16)
    for h in range(2):
        mixed[h, 0, 0, 0] = rows_in[h * rows:(h + 1) * rows]
    bias_row[...] = bias[...].reshape(1, hidden)
    head_row[...] = head[...].reshape(1, hidden)
    pl.semaphore_wait(barrier, len(partners))

    m_all = [Gather(mixed.at[h], nz, m_send.at[h], m_recv.at[h], dev) for h in range(2)]
    b_all = [Gather(big.at[h], nz, b_send.at[h], b_recv.at[h], dev) for h in range(2)]

    def block(held, dx, h):
        return held[h, dx].reshape(lot, feats)

    def arrived(held, send, recv, dx, h):
        for k in every:
            i = nz - 1 + dx * nz + k
            pltpu.make_async_remote_copy(
                src_ref=held.at[h, dx, k, 0], dst_ref=held.at[h, dx, k, 1],
                send_sem=send.at[h, i], recv_sem=recv.at[h, i],
                device_id=dev(0, 0, 1), device_id_type=MESH,
            ).wait_recv()

    def tiles(extent):
        return [pl.ds(i, tile) for i in range(0, extent, tile)]

    def hidden_units(dx, h):
        arrived(mixed, m_send, m_recv, dx, h)
        for cols in tiles(hidden):
            z = jnp.dot(block(mixed, dx, h), w[:, cols], preferred_element_type=f32)
            z = z + bias_row[:, cols]
            t = jnp.tanh(0.5 * z)
            sg = 0.5 + 0.5 * t
            slope = 0.25 * (1.0 - t * t)
            first = sg + z * slope
            second = slope * (2.0 - z * t)
            by = head_row[:, cols]
            d1[dx, h, :, cols] = first
            d2[dx, h, :, cols] = second * by
            u[dx, h, :, cols] = (first * by).astype(bf16)

    def pair_copy(h):
        return pltpu.make_async_remote_copy(
            src_ref=to_pair.at[h], dst_ref=from_pair.at[h], send_sem=p_send.at[h],
            recv_sem=p_recv.at[h], device_id=dev(0, 0, 1), device_id_type=MESH,
        )

    def z_copy(h, k):
        return pltpu.make_async_remote_copy(
            src_ref=to_z.at[h, k], dst_ref=from_z.at[h, k], send_sem=z_send.at[h, k],
            recv_sem=z_recv.at[h, k], device_id=dev(0, k, 0), device_id_type=MESH,
        )

    def input_gradient(h):
        for cols in tiles(feats):
            g = lax.dot_general(
                u[0, h], w[cols, :], (((1,), (1,)), ((), ())), preferred_element_type=f32
            ).reshape(nz, 2, rows, tile)
            for k in every:
                own[h, k, :, cols] = g[k, 0]
                to_pair[h, k, :, cols] = g[k, 1].astype(bf16)
        pair_copy(h).start()

    def pair_sum(h):
        pair_copy(h).wait_recv()
        for k in others + (0,):
            both = own[h, k] + from_pair[h, k].astype(f32)
            if k:
                to_z[h, k] = both.astype(bf16)
                z_copy(h, k).start()
            else:
                own[h, 0] = both

    def scale_rows(h):
        g = own[h, 0]
        for k in others:
            z_copy(h, k).wait_recv()
            g = g + from_z[h, k].astype(f32)
        norm = jnp.sqrt(jnp.sum(g * g, axis=1, keepdims=True) + 1e-06)
        big[h, 0, 0, 0] = (20.0 * (norm - 1.0) / norm * g).astype(bf16)
        b_all[h].start()
        return jnp.sum((norm - 1.0) ** 2, axis=0, keepdims=True)

    def weight_terms(dx, h):
        arrived(big, b_send, b_recv, dx, h)
        mine = pl.ds(pl.multiple_of(dp * part, 128), part)
        for j, held in enumerate((mixed, big)):
            lhs[j] = held[h, dx, :, :, :, mine].reshape(lot, part).T
        for cols in tiles(hidden):
            p = jnp.dot(block(big, dx, h), w[:, cols], preferred_element_type=f32)
            dz = p * d2[dx, h, :, cols]
            ph = p * d1[dx, h, :, cols]
            sum_bias[h, dx, :, cols] = jnp.sum(dz.reshape(lot // 8, 8, tile), axis=0)
            sum_head[h, dx, :, cols] = jnp.sum(ph.reshape(lot // 8, 8, tile), axis=0)
            term = jnp.dot(lhs[0], dz.astype(bf16), preferred_element_type=f32)
            term = term + jnp.dot(lhs[1], u[dx, h, :, cols], preferred_element_type=f32)
            out[:, cols] += term

    hops = [dev(0, 0, 1)]
    bit = 1
    while bit < nz:
        hops.append(dev(0, bit, 0))
        bit *= 2
    hops += [dev(1, 0, 0), dev(2, 0, 0)]

    def loss_copy(i):
        return pltpu.make_async_remote_copy(
            src_ref=loss.at[i], dst_ref=loss_in.at[i], send_sem=l_send.at[i],
            recv_sem=l_recv.at[i], device_id=hops[i], device_id_type=MESH,
        )

    def loss_step(i):
        loss_copy(i).wait_recv()
        loss[i + 1] = loss[i] + loss_in[i]
        if i + 1 < len(hops):
            loss_copy(i + 1).start()

    m_all[0].start()
    m_all[1].start()
    load_w.wait()
    m_all[0].spread(*others)

    def after_hidden(n):
        if n == 0:
            m_all[0].turn(*every)
        elif n == 1:
            pair_sum(0)
            m_all[1].spread(*others)
        elif n == 2:
            m_all[0].last(*every)
        elif n == 3:
            pair_sum(1)
            loss[0] = jnp.broadcast_to(scale_rows(0), loss.shape[1:])
        elif n == 4:
            b_all[0].spread(1)
            m_all[1].turn(*every)
        elif n == 5:
            b_all[0].spread(*others[1:])
        elif n == 6:
            loss[0] += jnp.broadcast_to(scale_rows(1), loss.shape[1:])
            loss_copy(0).start()
            m_all[1].last(*every)
            b_all[0].turn(*every[:2])
        else:
            loss_step(0)
            b_all[0].turn(*every[2:])
            b_all[1].spread(1)

    order = ((0, 0), (1, 0), (0, 1), (2, 0), (3, 0), (1, 1), (2, 1), (3, 1))

    def hidden_step(n, carry):
        dx, h = n * 0, n * 0
        for i, (group, half) in enumerate(order):
            dx = jnp.where(n == i, group, dx)
            h = jnp.where(n == i, half, h)
        hidden_units(dx, h)

        @pl.when(jnp.logical_or(n == 0, n == 2))
        def _():
            input_gradient(h)

        for i in range(len(order)):
            pl.when(n == i)(functools.partial(after_hidden, i))
        return carry

    lax.fori_loop(0, len(order), hidden_step, 0)

    out[...] = jnp.zeros_like(out)

    def before_weights(n):
        if n == 0:
            b_all[1].spread(*others[1:])
        elif n == 2:
            b_all[0].last(*every)
            b_all[1].turn(*every[:2])
        elif n == 3:
            b_all[1].turn(*every[2:])
        elif n == 5:
            b_all[1].last(*every)
        if n + 1 < len(hops):
            loss_step(n + 1)

    def weight_step(n, carry):
        for i in range(len(order)):
            pl.when(n == i)(functools.partial(before_weights, i))
        weight_terms(lax.rem(n, 4), n // 4)
        return carry

    lax.fori_loop(0, len(order), weight_step, 0)
    for i in range(len(order) + 1, len(hops)):
        loss_step(i)

    for ref, sums in ((out_bias, sum_bias), (out_head, sum_head)):
        part_sums = [sums[0, dx] + sums[1, dx] for dx in range(4)]
        whole = (part_sums[0] + part_sums[1]) + (part_sums[2] + part_sums[3])
        ref[...] = jnp.sum(whole, axis=0, keepdims=True).reshape(hidden)
    out_pen[0, 0] = (10.0 * loss[len(hops)] / total_rows)[0, 0]

    for h in range(2):
        m_all[h].finish()
        b_all[h].finish()
        pair_copy(h).wait_send()
        for k in others:
            z_copy(h, k).wait_send()
    for i in range(len(hops)):
        loss_copy(i).wait_send()


def scratch_of(rows, feats, hidden, part, nz):
    f32, bf16 = jnp.float32, jnp.bfloat16
    hops = nz.bit_length() + 2
    lot = nz * rows
    held = [
        ((feats, hidden), bf16),
        ((2, 4, nz, 2, rows // 2, feats), bf16),
        ((2, 4, nz, 2, rows // 2, feats), bf16),
        ((4, 2, lot, hidden), bf16),
        ((4, 2, lot, hidden), f32),
        ((4, 2, lot, hidden), f32),
        ((2, nz, rows // 2, feats), f32),
        ((2, part, lot), bf16),
        ((2, nz, rows // 2, feats), bf16),
        ((2, nz, rows // 2, feats), bf16),
        ((2, nz, rows // 2, feats), bf16),
        ((2, nz, rows // 2, feats), bf16),
        ((2, 4, 8, hidden), f32),
        ((2, 4, 8, hidden), f32),
        ((hops + 1, 8, 128), f32),
        ((hops + 1, 8, 128), f32),
        ((1, hidden), f32),
        ((1, hidden), f32),
    ]
    moves = nz - 1 + 8 * nz
    sems = [(), (2, moves), (2, moves), (2, moves), (2, moves), (2,), (2,), (2, nz), (2, nz), (hops,), (hops,)]
    return held, sems


def solution(mesh):
    placed = (
        P(("dp", "tensor"), None),
        P(("dp", "tensor"), None),
        P(("dp", "tensor")),
        P(None, "tensor"),
        P("tensor"),
        P("tensor"),
    )
    groups, members = mesh.shape["dp"], mesh.shape["tensor"]
    nz = members // 2

    def body(real_feats, fake_feats, mix_num, w_first, bias, head):
        rows, feats = real_feats.shape
        hidden = w_first.shape[1]
        part = feats // groups
        held, sems = scratch_of(rows, feats, hidden, part, max(nz, 2))
        size = part * hidden * 4
        for shape, dtype in held:
            size += functools.reduce(lambda a, b: a * b, shape) * jnp.dtype(dtype).itemsize
        tile = next((t for t in (256, 128) if hidden % t == 0 and feats % t == 0), 0)
        fits = (
            groups == 4 and members % 2 == 0 and nz >= 2 and nz & (nz - 1) == 0
            and tile and rows % 64 == 0 and part % 128 == 0 and size <= HELD_BYTES
        )
        if not fits:
            return local(real_feats, fake_feats, mix_num, w_first, bias, head)
        vmem = pl.BlockSpec(memory_space=pltpu.VMEM)
        total_rows = rows * groups * members
        grad_w, grad_bias, grad_head, pen = pl.pallas_call(
            functools.partial(kernel, nz, tile, total_rows),
            out_shape=(
                jax.ShapeDtypeStruct((part, hidden), jnp.float32),
                jax.ShapeDtypeStruct((hidden,), jnp.float32),
                jax.ShapeDtypeStruct((hidden,), jnp.float32),
                jax.ShapeDtypeStruct((1, 1), jnp.float32),
            ),
            in_specs=[vmem, vmem, vmem, pl.BlockSpec(memory_space=pl.ANY), vmem, vmem],
            out_specs=(vmem, vmem, vmem, pl.BlockSpec(memory_space=pltpu.SMEM)),
            scratch_shapes=[pltpu.VMEM(s, t) for s, t in held]
            + [pltpu.SemaphoreType.DMA(s) if s else pltpu.SemaphoreType.DMA for s in sems],
            compiler_params=pltpu.CompilerParams(
                collective_id=0, has_side_effects=True, vmem_limit_bytes=VMEM_BYTES
            ),
        )(real_feats, fake_feats, mix_num, w_first, bias, head)
        return (grad_w, grad_bias, grad_head, pen.reshape(()))

    return jax.shard_map(
        body,
        mesh=mesh,
        in_specs=placed,
        out_specs=(P("dp", "tensor"), P("tensor"), P("tensor"), P()),
        check_vma=False,
    )
```

```python
import functools

import jax
import jax.numpy as jnp
from jax import lax
from jax.experimental import pallas as pl
from jax.experimental.pallas import tpu as pltpu
from jax.sharding import PartitionSpec as P

MESH = pl.DeviceIdType.MESH
VMEM_BYTES = 63 * 2**20
HELD_BYTES = 61 * 2**20


def row_contract(left, right):
    return lax.dot_general(
        left, right, (((0,), (0,)), ((), ())), preferred_element_type=jnp.float32
    )


def local(real_feats, fake_feats, mix_num, w_first, bias, head):
    coef = mix_num.astype(jnp.float32) / 256.0
    real_f = real_feats.astype(jnp.float32)
    mixed = (real_f + coef[:, None] * (fake_feats.astype(jnp.float32) - real_f)).astype(
        jnp.bfloat16
    )
    group = lax.all_gather(mixed, "tensor", axis=0, tiled=True)
    z = jnp.dot(group, w_first, preferred_element_type=jnp.float32) + bias
    sg = jax.nn.sigmoid(z)
    d1 = sg * (1.0 + z * (1.0 - sg))
    d2 = sg * (1.0 - sg) * (2.0 + z * (1.0 - 2.0 * sg))
    u = (d1 * head).astype(jnp.bfloat16)
    total_rows = group.shape[0] * lax.axis_size("dp")
    grad_in = lax.psum_scatter(
        lax.dot_general(
            u, w_first, (((1,), (1,)), ((), ())), preferred_element_type=jnp.float32
        ).astype(jnp.bfloat16),
        "tensor",
        scatter_dimension=0,
        tiled=True,
    ).astype(jnp.float32)
    norm = jnp.sqrt(jnp.sum(grad_in * grad_in, axis=1) + 1e-06)
    scale = 20.0 * (norm - 1.0) / norm
    scaled = (scale[:, None] * grad_in).astype(jnp.bfloat16)
    loss = lax.psum(jnp.sum((norm - 1.0) ** 2), ("dp", "tensor"))
    big = lax.all_gather(scaled, "tensor", axis=0, tiled=True)
    penalty = 10.0 * loss / total_rows
    p = jnp.dot(big, w_first, preferred_element_type=jnp.float32)
    dz = p * head * d2
    dzb = dz.astype(jnp.bfloat16)
    partial_w = row_contract(group, dzb)
    partial_w = partial_w + row_contract(big, u)
    grad_w = lax.psum_scatter(partial_w, "dp", scatter_dimension=0, tiled=True)
    grad_bias, grad_head = lax.psum((jnp.sum(dz, axis=0), jnp.sum(p * d1, axis=0)), "dp")
    return (grad_w, grad_bias, grad_head, penalty)


def flip(index, mask):
    bit = 1
    while bit <= mask:
        if mask & bit:
            index = index + bit - 2 * bit * lax.rem(index // bit, 2)
        bit *= 2
    return index


class Gather:
    def __init__(self, held, nz, send, recv, dev):
        self.held, self.nz, self.dev = held, nz, dev
        self.send, self.recv = send, recv
        self.names = (
            [("z", 0, k) for k in range(1, nz)]
            + [(kind, dx, k) for kind, dxs in (("c", range(4)), ("xy", (1, 2)), ("d", (0, 1)))
               for dx in dxs for k in range(nz)]
        )

    def copy(self, name):
        kind, dx, k = name
        held, dev = self.held, self.dev
        half = held.shape[3] // 2
        if kind == "z":
            src, dst, to = held.at[0, 0, 0], held.at[0, k, 0], dev(0, k, 0)
        elif kind == "c":
            src, dst, to = held.at[dx, k, 0], held.at[dx, k, 1], dev(0, 0, 1)
        elif kind == "xy":
            src, dst, to = held.at[0, k, 0], held.at[dx, k, 0], dev(dx, 0, 0)
        else:
            rows = pl.ds(dx * half, half)
            src, dst, to = held.at[1 + dx, k, 0, rows], held.at[3, k, 0, rows], dev(2 - dx, 0, 0)
        i = self.names.index(name)
        return pltpu.make_async_remote_copy(
            src_ref=src, dst_ref=dst, send_sem=self.send.at[i], recv_sem=self.recv.at[i],
            device_id=to, device_id_type=MESH,
        )

    def start(self):
        for k in range(1, self.nz):
            self.copy(("z", 0, k)).start()
        self.spread(0)

    def spread(self, *ks):
        for k in ks:
            if k:
                self.copy(("z", 0, k)).wait_recv()
            for name in (("xy", 1, k), ("xy", 2, k), ("c", 0, k)):
                self.copy(name).start()

    def turn(self, *ks):
        for k in ks:
            for dx in (1, 2):
                self.copy(("xy", dx, k)).wait_recv()
                self.copy(("d", dx - 1, k)).start()
                self.copy(("c", dx, k)).start()

    def last(self, *ks):
        for k in ks:
            self.copy(("d", 0, k)).wait_recv()
            self.copy(("d", 1, k)).wait_recv()
            self.copy(("c", 3, k)).start()

    def finish(self):
        for name in self.names:
            self.copy(name).wait_send()


def kernel(
    nz, tile, total_rows,
    real, fake, mix, w_hbm, bias, head,
    out, out_bias, out_head, out_pen,
    w, w_t, mixed, big, u, d1, d2, own, to_pair, from_pair, to_z, from_z,
    sums, loss, loss_in, bias_col, head_col,
    w_sem, m_send, m_recv, b_send, b_recv, p_send, p_recv, z_send, z_recv, l_send, l_recv,
):
    f32, bf16 = jnp.float32, jnp.bfloat16
    dp, tensor = lax.axis_index("dp"), lax.axis_index("tensor")
    z_at, core = tensor // 2, lax.rem(tensor, 2)
    feats = real.shape[1]
    rows = real.shape[0] // 2
    lot = 2 * nz * rows
    hidden = w.shape[1]
    part = out.shape[1]
    every, others = tuple(range(nz)), tuple(range(1, nz))

    def dev(dx, zx, cc):
        return (flip(dp, dx), flip(z_at, zx) * 2 + flip(core, cc))

    load_w = pltpu.make_async_copy(w_hbm, w, w_sem)
    load_w.start()
    partners = [dev(0, 0, 1), dev(1, 0, 0), dev(2, 0, 0)]
    partners += [dev(0, k, 0) for k in others]
    barrier = pltpu.get_barrier_semaphore()
    for to in partners:
        pl.semaphore_signal(barrier, inc=1, device_id=to, device_id_type=MESH)
    count = mix.shape[0]
    places = [lax.broadcasted_iota(jnp.int32, (count, count), axis) for axis in (0, 1)]
    spread = jnp.broadcast_to(mix[...].reshape(1, count).astype(f32), (count, count))
    spread = jnp.where(places[0] == places[1], spread, 0.0)
    coef = jnp.sum(spread, axis=1, keepdims=True) / 256.0
    real_f = real[...].astype(f32)
    rows_in = (real_f + coef * (fake[...].astype(f32) - real_f)).astype(bf16)
    for h in range(2):
        mixed[h, 0, 0, 0] = rows_in[h * rows:(h + 1) * rows]
    pl.semaphore_wait(barrier, len(partners))

    m_all = [Gather(mixed.at[h], nz, m_send.at[h], m_recv.at[h], dev) for h in range(2)]
    b_all = [Gather(big.at[h], nz, b_send.at[h], b_recv.at[h], dev) for h in range(2)]

    def block(held, dx, h):
        return held[h, dx].reshape(lot, feats)

    def arrived(held, send, recv, dx, h):
        for k in every:
            i = nz - 1 + dx * nz + k
            pltpu.make_async_remote_copy(
                src_ref=held.at[h, dx, k, 0], dst_ref=held.at[h, dx, k, 1],
                send_sem=send.at[h, i], recv_sem=recv.at[h, i],
                device_id=dev(0, 0, 1), device_id_type=MESH,
            ).wait_recv()

    def tiles(extent, size=tile):
        return [pl.ds(i, size) for i in range(0, extent, size)]

    def across(col, units):
        return jnp.concatenate([col[units, :]] * (lot // 128), axis=1)

    def product(left, right):
        return lax.dot_general(
            left, right, (((1,), (1,)), ((), ())), preferred_element_type=f32
        )

    def hidden_units(dx, h):
        arrived(mixed, m_send, m_recv, dx, h)
        for units in tiles(hidden):
            z = product(w_t[units, :], block(mixed, dx, h))
            z = z + across(bias_col, units)
            t = jnp.tanh(0.5 * z)
            sg = 0.5 + 0.5 * t
            slope = 0.25 * (1.0 - t * t)
            first = sg + z * slope
            second = slope * (2.0 - z * t)
            by = across(head_col, units)
            d1[dx, h, units, :] = first
            d2[dx, h, units, :] = second * by
            u[dx, h, units, :] = (first * by).astype(bf16)

    def pair_copy(h):
        return pltpu.make_async_remote_copy(
            src_ref=to_pair.at[h], dst_ref=from_pair.at[h], send_sem=p_send.at[h],
            recv_sem=p_recv.at[h], device_id=dev(0, 0, 1), device_id_type=MESH,
        )

    def z_copy(h, k):
        return pltpu.make_async_remote_copy(
            src_ref=to_z.at[h, k], dst_ref=from_z.at[h, k], send_sem=z_send.at[h, k],
            recv_sem=z_recv.at[h, k], device_id=dev(0, k, 0), device_id_type=MESH,
        )

    def input_gradient(h):
        for cols in tiles(feats):
            g = jnp.dot(w[cols, :], u[0, h], preferred_element_type=f32).T
            g = g.reshape(nz, 2, rows, tile)
            for k in every:
                own[h, k, :, cols] = g[k, 0]
                to_pair[h, k, :, cols] = g[k, 1].astype(bf16)
        pair_copy(h).start()

    def pair_sum(h):
        pair_copy(h).wait_recv()
        for k in others + (0,):
            both = own[h, k] + from_pair[h, k].astype(f32)
            if k:
                to_z[h, k] = both.astype(bf16)
                z_copy(h, k).start()
            else:
                own[h, 0] = both

    def scale_rows(h):
        g = own[h, 0]
        for k in others:
            z_copy(h, k).wait_recv()
            g = g + from_z[h, k].astype(f32)
        norm = jnp.sqrt(jnp.sum(g * g, axis=1, keepdims=True) + 1e-06)
        big[h, 0, 0, 0] = (20.0 * (norm - 1.0) / norm * g).astype(bf16)
        b_all[h].start()
        return jnp.sum((norm - 1.0) ** 2, axis=0, keepdims=True)

    def weight_terms(dx, h):
        arrived(big, b_send, b_recv, dx, h)
        mine = pl.ds(pl.multiple_of(dp * part, 128), part)
        mixed_part = mixed[h, dx, :, :, :, mine].reshape(lot, part)
        big_part = big[h, dx, :, :, :, mine].reshape(lot, part)
        for units in tiles(hidden):
            p = product(w_t[units, :], block(big, dx, h))
            dz = p * d2[dx, h, units, :]
            ph = p * d1[dx, h, units, :]
            lane = lax.broadcasted_iota(jnp.int32, (tile, 128), 1)
            row = sums[units, :]
            row = jnp.where(lane == 2 * dx + h, jnp.sum(dz, axis=1, keepdims=True), row)
            row = jnp.where(lane == 8 + 2 * dx + h, jnp.sum(ph, axis=1, keepdims=True), row)
            sums[units, :] = row
            term = jnp.dot(dz.astype(bf16), mixed_part, preferred_element_type=f32)
            term = term + jnp.dot(u[dx, h, units, :], big_part, preferred_element_type=f32)
            out[units, :] += term

    hops = [dev(0, 0, 1)]
    bit = 1
    while bit < nz:
        hops.append(dev(0, bit, 0))
        bit *= 2
    hops += [dev(1, 0, 0), dev(2, 0, 0)]

    def loss_copy(i):
        return pltpu.make_async_remote_copy(
            src_ref=loss.at[i], dst_ref=loss_in.at[i], send_sem=l_send.at[i],
            recv_sem=l_recv.at[i], device_id=hops[i], device_id_type=MESH,
        )

    def loss_step(i):
        loss_copy(i).wait_recv()
        loss[i + 1] = loss[i] + loss_in[i]
        if i + 1 < len(hops):
            loss_copy(i + 1).start()

    m_all[0].start()
    m_all[1].start()
    for ref, col in ((bias, bias_col), (head, head_col)):
        col[...] = jnp.broadcast_to(ref[...].reshape(1, hidden), (128, hidden)).T
    load_w.wait()
    for cols in tiles(hidden, 256):
        w_t[cols, :] = w[:, cols].T
    m_all[0].spread(*others)

    def after_hidden(n):
        if n == 0:
            m_all[0].turn(*every)
        elif n == 1:
            pair_sum(0)
            m_all[1].spread(*others)
        elif n == 2:
            m_all[0].last(*every)
        elif n == 3:
            pair_sum(1)
            loss[0] = jnp.broadcast_to(scale_rows(0), loss.shape[1:])
        elif n == 4:
            b_all[0].spread(1)
            m_all[1].turn(*every)
        elif n == 5:
            b_all[0].spread(*others[1:])
        elif n == 6:
            loss[0] += jnp.broadcast_to(scale_rows(1), loss.shape[1:])
            loss_copy(0).start()
            m_all[1].last(*every)
            b_all[0].turn(*every[:2])
        else:
            loss_step(0)
            b_all[0].turn(*every[2:])
            b_all[1].spread(1)

    order = ((0, 0), (1, 0), (0, 1), (2, 0), (3, 0), (1, 1), (2, 1), (3, 1))

    def hidden_step(n, carry):
        dx, h = n * 0, n * 0
        for i, (group, half) in enumerate(order):
            dx = jnp.where(n == i, group, dx)
            h = jnp.where(n == i, half, h)
        hidden_units(dx, h)

        @pl.when(jnp.logical_or(n == 0, n == 2))
        def _():
            input_gradient(h)

        for i in range(len(order)):
            pl.when(n == i)(functools.partial(after_hidden, i))
        return carry

    lax.fori_loop(0, len(order), hidden_step, 0)

    out[...] = jnp.zeros_like(out)
    sums[...] = jnp.zeros_like(sums)

    def before_weights(n):
        if n == 0:
            b_all[1].spread(*others[1:])
        elif n == 2:
            b_all[0].last(*every)
            b_all[1].turn(*every[:2])
        elif n == 3:
            b_all[1].turn(*every[2:])
        elif n == 5:
            b_all[1].last(*every)
        if n + 1 < len(hops):
            loss_step(n + 1)

    def weight_step(n, carry):
        for i in range(len(order)):
            pl.when(n == i)(functools.partial(before_weights, i))
        weight_terms(lax.rem(n, 4), n // 4)
        return carry

    lax.fori_loop(0, len(order), weight_step, 0)
    for i in range(len(order) + 1, len(hops)):
        loss_step(i)

    by_lot = sums[...].T
    for ref, first in ((out_bias, 0), (out_head, 8)):
        group = [by_lot[first + i:first + i + 1] + by_lot[first + i + 1:first + i + 2] for i in (0, 2, 4, 6)]
        ref[...] = ((group[0] + group[1]) + (group[2] + group[3])).reshape(hidden)
    out_pen[0, 0] = (10.0 * loss[len(hops)] / total_rows)[0, 0]

    for h in range(2):
        m_all[h].finish()
        b_all[h].finish()
        pair_copy(h).wait_send()
        for k in others:
            z_copy(h, k).wait_send()
    for i in range(len(hops)):
        loss_copy(i).wait_send()


def scratch_of(rows, feats, hidden, part, nz):
    f32, bf16 = jnp.float32, jnp.bfloat16
    hops = nz.bit_length() + 2
    lot = nz * rows
    held = [
        ((feats, hidden), bf16),
        ((hidden, feats), bf16),
        ((2, 4, nz, 2, rows // 2, feats), bf16),
        ((2, 4, nz, 2, rows // 2, feats), bf16),
        ((4, 2, hidden, lot), bf16),
        ((4, 2, hidden, lot), f32),
        ((4, 2, hidden, lot), f32),
        ((2, nz, rows // 2, feats), f32),
        ((2, nz, rows // 2, feats), bf16),
        ((2, nz, rows // 2, feats), bf16),
        ((2, nz, rows // 2, feats), bf16),
        ((2, nz, rows // 2, feats), bf16),
        ((hidden, 128), f32),
        ((hops + 1, 8, 128), f32),
        ((hops + 1, 8, 128), f32),
        ((hidden, 128), f32),
        ((hidden, 128), f32),
    ]
    moves = nz - 1 + 8 * nz
    sems = [(), (2, moves), (2, moves), (2, moves), (2, moves), (2,), (2,), (2, nz), (2, nz), (hops,), (hops,)]
    return held, sems


def solution(mesh):
    placed = (
        P(("dp", "tensor"), None),
        P(("dp", "tensor"), None),
        P(("dp", "tensor")),
        P(None, "tensor"),
        P("tensor"),
        P("tensor"),
    )
    groups, members = mesh.shape["dp"], mesh.shape["tensor"]
    nz = members // 2

    def body(real_feats, fake_feats, mix_num, w_first, bias, head):
        rows, feats = real_feats.shape
        hidden = w_first.shape[1]
        part = feats // groups
        held, sems = scratch_of(rows, feats, hidden, part, max(nz, 2))
        size = part * hidden * 4
        for shape, dtype in held:
            size += functools.reduce(lambda a, b: a * b, shape) * jnp.dtype(dtype).itemsize
        tile = next((t for t in (768, 512, 256) if hidden % t == 0 and feats % t == 0), 0)
        fits = (
            groups == 4 and members % 2 == 0 and nz >= 2 and nz & (nz - 1) == 0
            and tile and rows % 64 == 0 and nz * rows % 128 == 0 and part % 128 == 0 and size <= HELD_BYTES
        )
        if not fits:
            return local(real_feats, fake_feats, mix_num, w_first, bias, head)
        vmem = pl.BlockSpec(memory_space=pltpu.VMEM)
        total_rows = rows * groups * members
        grad_w, grad_bias, grad_head, pen = pl.pallas_call(
            functools.partial(kernel, nz, tile, total_rows),
            out_shape=(
                jax.ShapeDtypeStruct((hidden, part), jnp.float32),
                jax.ShapeDtypeStruct((hidden,), jnp.float32),
                jax.ShapeDtypeStruct((hidden,), jnp.float32),
                jax.ShapeDtypeStruct((1, 1), jnp.float32),
            ),
            in_specs=[vmem, vmem, vmem, pl.BlockSpec(memory_space=pl.ANY), vmem, vmem],
            out_specs=(vmem, vmem, vmem, pl.BlockSpec(memory_space=pltpu.SMEM)),
            scratch_shapes=[pltpu.VMEM(s, t) for s, t in held]
            + [pltpu.SemaphoreType.DMA(s) if s else pltpu.SemaphoreType.DMA for s in sems],
            compiler_params=pltpu.CompilerParams(
                collective_id=0, has_side_effects=True, vmem_limit_bytes=VMEM_BYTES
            ),
        )(real_feats, fake_feats, mix_num, w_first, bias, head)
        return (grad_w.T, grad_bias, grad_head, pen.reshape(()))

    return jax.shard_map(
        body,
        mesh=mesh,
        in_specs=placed,
        out_specs=(P("dp", "tensor"), P("tensor"), P("tensor"), P()),
        check_vma=False,
    )
```

```python
import functools

import jax
import jax.numpy as jnp
from jax import lax
from jax.experimental import pallas as pl
from jax.experimental.pallas import tpu as pltpu
from jax.sharding import PartitionSpec as P

MESH = pl.DeviceIdType.MESH
VMEM_BYTES = 63 * 2**20
HELD_BYTES = 61 * 2**20


def row_contract(left, right):
    return lax.dot_general(
        left, right, (((0,), (0,)), ((), ())), preferred_element_type=jnp.float32
    )


def local(real_feats, fake_feats, mix_num, w_first, bias, head):
    coef = mix_num.astype(jnp.float32) / 256.0
    real_f = real_feats.astype(jnp.float32)
    mixed = (real_f + coef[:, None] * (fake_feats.astype(jnp.float32) - real_f)).astype(
        jnp.bfloat16
    )
    group = lax.all_gather(mixed, "tensor", axis=0, tiled=True)
    z = jnp.dot(group, w_first, preferred_element_type=jnp.float32) + bias
    sg = jax.nn.sigmoid(z)
    d1 = sg * (1.0 + z * (1.0 - sg))
    d2 = sg * (1.0 - sg) * (2.0 + z * (1.0 - 2.0 * sg))
    u = (d1 * head).astype(jnp.bfloat16)
    total_rows = group.shape[0] * lax.axis_size("dp")
    grad_in = lax.psum_scatter(
        lax.dot_general(
            u, w_first, (((1,), (1,)), ((), ())), preferred_element_type=jnp.float32
        ).astype(jnp.bfloat16),
        "tensor",
        scatter_dimension=0,
        tiled=True,
    ).astype(jnp.float32)
    norm = jnp.sqrt(jnp.sum(grad_in * grad_in, axis=1) + 1e-06)
    scale = 20.0 * (norm - 1.0) / norm
    scaled = (scale[:, None] * grad_in).astype(jnp.bfloat16)
    loss = lax.psum(jnp.sum((norm - 1.0) ** 2), ("dp", "tensor"))
    big = lax.all_gather(scaled, "tensor", axis=0, tiled=True)
    penalty = 10.0 * loss / total_rows
    p = jnp.dot(big, w_first, preferred_element_type=jnp.float32)
    dz = p * head * d2
    dzb = dz.astype(jnp.bfloat16)
    partial_w = row_contract(group, dzb)
    partial_w = partial_w + row_contract(big, u)
    grad_w = lax.psum_scatter(partial_w, "dp", scatter_dimension=0, tiled=True)
    grad_bias, grad_head = lax.psum((jnp.sum(dz, axis=0), jnp.sum(p * d1, axis=0)), "dp")
    return (grad_w, grad_bias, grad_head, penalty)


def flip(index, mask):
    bit = 1
    while bit <= mask:
        if mask & bit:
            index = index + bit - 2 * bit * lax.rem(index // bit, 2)
        bit *= 2
    return index


class Gather:
    def __init__(self, held, nz, send, recv, dev):
        self.held, self.nz, self.dev = held, nz, dev
        self.send, self.recv = send, recv
        self.names = (
            [("z", 0, k) for k in range(1, nz)]
            + [(kind, dx, k) for kind, dxs in (("c", range(4)), ("xy", (1, 2)), ("d", (0, 1)))
               for dx in dxs for k in range(nz)]
        )

    def copy(self, name):
        kind, dx, k = name
        held, dev = self.held, self.dev
        half = held.shape[3] // 2
        if kind == "z":
            src, dst, to = held.at[0, 0, 0], held.at[0, k, 0], dev(0, k, 0)
        elif kind == "c":
            src, dst, to = held.at[dx, k, 0], held.at[dx, k, 1], dev(0, 0, 1)
        elif kind == "xy":
            src, dst, to = held.at[0, k, 0], held.at[dx, k, 0], dev(dx, 0, 0)
        else:
            rows = pl.ds(dx * half, half)
            src, dst, to = held.at[1 + dx, k, 0, rows], held.at[3, k, 0, rows], dev(2 - dx, 0, 0)
        i = self.names.index(name)
        return pltpu.make_async_remote_copy(
            src_ref=src, dst_ref=dst, send_sem=self.send.at[i], recv_sem=self.recv.at[i],
            device_id=to, device_id_type=MESH,
        )

    def start(self):
        for k in range(1, self.nz):
            self.copy(("z", 0, k)).start()
        self.spread(0)

    def spread(self, *ks):
        for k in ks:
            if k:
                self.copy(("z", 0, k)).wait_recv()
            for name in (("xy", 1, k), ("xy", 2, k), ("c", 0, k)):
                self.copy(name).start()

    def turn(self, *ks):
        for k in ks:
            for dx in (1, 2):
                self.copy(("xy", dx, k)).wait_recv()
                self.copy(("d", dx - 1, k)).start()
                self.copy(("c", dx, k)).start()

    def last(self, *ks):
        for k in ks:
            self.copy(("d", 0, k)).wait_recv()
            self.copy(("d", 1, k)).wait_recv()
            self.copy(("c", 3, k)).start()

    def finish(self):
        for name in self.names:
            self.copy(name).wait_send()


def kernel(
    nz, tile, total_rows,
    real, fake, mix, w_hbm, bias, head,
    out, out_bias, out_head, out_pen,
    w, w_t, mixed, big, u, d1, d2, own, to_pair, from_pair, to_z, from_z,
    sums, loss, loss_in, bias_col, head_col,
    w_sem, m_send, m_recv, b_send, b_recv, p_send, p_recv, z_send, z_recv, l_send, l_recv,
):
    f32, bf16 = jnp.float32, jnp.bfloat16
    dp, tensor = lax.axis_index("dp"), lax.axis_index("tensor")
    z_at, core = tensor // 2, lax.rem(tensor, 2)
    feats = real.shape[1]
    rows = real.shape[0] // 2
    lot = 2 * nz * rows
    hidden = w.shape[1]
    part = out.shape[1]
    every, others = tuple(range(nz)), tuple(range(1, nz))

    def dev(dx, zx, cc):
        return (flip(dp, dx), flip(z_at, zx) * 2 + flip(core, cc))

    load_w = pltpu.make_async_copy(w_hbm, w, w_sem)
    load_w.start()
    partners = [dev(0, 0, 1), dev(1, 0, 0), dev(2, 0, 0)]
    partners += [dev(0, k, 0) for k in others]
    barrier = pltpu.get_barrier_semaphore()
    for to in partners:
        pl.semaphore_signal(barrier, inc=1, device_id=to, device_id_type=MESH)
    count = mix.shape[0]
    places = [lax.broadcasted_iota(jnp.int32, (count, count), axis) for axis in (0, 1)]
    spread = jnp.broadcast_to(mix[...].reshape(1, count).astype(f32), (count, count))
    spread = jnp.where(places[0] == places[1], spread, 0.0)
    coef = jnp.sum(spread, axis=1, keepdims=True) / 256.0
    real_f = real[...].astype(f32)
    rows_in = (real_f + coef * (fake[...].astype(f32) - real_f)).astype(bf16)
    for h in range(2):
        mixed[h, 0, 0, 0] = rows_in[h * rows:(h + 1) * rows]
    pl.semaphore_wait(barrier, len(partners))

    m_all = [Gather(mixed.at[h], nz, m_send.at[h], m_recv.at[h], dev) for h in range(2)]
    b_all = [Gather(big.at[h], nz, b_send.at[h], b_recv.at[h], dev) for h in range(2)]

    def block(held, dx, h):
        return held[h, dx].reshape(lot, feats)

    def arrived(held, send, recv, dx, h):
        for k in every:
            i = nz - 1 + dx * nz + k
            pltpu.make_async_remote_copy(
                src_ref=held.at[h, dx, k, 0], dst_ref=held.at[h, dx, k, 1],
                send_sem=send.at[h, i], recv_sem=recv.at[h, i],
                device_id=dev(0, 0, 1), device_id_type=MESH,
            ).wait_recv()

    def tiles(extent, size=tile):
        def over(step):
            def turn(i, carry):
                step(pl.ds(pl.multiple_of(i * size, size), size))
                return carry

            lax.fori_loop(0, extent // size, turn, 0)

        return over

    def across(col, units):
        return jnp.concatenate([col[units, :]] * (lot // 128), axis=1)

    def product(left, right):
        return lax.dot_general(
            left, right, (((1,), (1,)), ((), ())), preferred_element_type=f32
        )

    def hidden_units(dx, h):
        arrived(mixed, m_send, m_recv, dx, h)
        @tiles(hidden)
        def _(units):
            z = product(w_t[units, :], block(mixed, dx, h))
            z = z + across(bias_col, units)
            t = jnp.tanh(0.5 * z)
            sg = 0.5 + 0.5 * t
            slope = 0.25 * (1.0 - t * t)
            first = sg + z * slope
            second = slope * (2.0 - z * t)
            by = across(head_col, units)
            d1[dx, h, units, :] = first
            d2[dx, h, units, :] = second * by
            u[dx, h, units, :] = (first * by).astype(bf16)

    def pair_copy(h):
        return pltpu.make_async_remote_copy(
            src_ref=to_pair.at[h], dst_ref=from_pair.at[h], send_sem=p_send.at[h],
            recv_sem=p_recv.at[h], device_id=dev(0, 0, 1), device_id_type=MESH,
        )

    def z_copy(h, k):
        return pltpu.make_async_remote_copy(
            src_ref=to_z.at[h, k], dst_ref=from_z.at[h, k], send_sem=z_send.at[h, k],
            recv_sem=z_recv.at[h, k], device_id=dev(0, k, 0), device_id_type=MESH,
        )

    def input_gradient(h):
        @tiles(feats)
        def _(cols):
            g = jnp.dot(w[cols, :], u[0, h], preferred_element_type=f32).T
            g = g.reshape(nz, 2, rows, tile)
            for k in every:
                own[h, k, :, cols] = g[k, 0]
                to_pair[h, k, :, cols] = g[k, 1].astype(bf16)

        pair_copy(h).start()

    def pair_sum(h):
        pair_copy(h).wait_recv()
        for k in others + (0,):
            both = own[h, k] + from_pair[h, k].astype(f32)
            if k:
                to_z[h, k] = both.astype(bf16)
                z_copy(h, k).start()
            else:
                own[h, 0] = both

    def scale_rows(h):
        g = own[h, 0]
        for k in others:
            z_copy(h, k).wait_recv()
            g = g + from_z[h, k].astype(f32)
        norm = jnp.sqrt(jnp.sum(g * g, axis=1, keepdims=True) + 1e-06)
        big[h, 0, 0, 0] = (20.0 * (norm - 1.0) / norm * g).astype(bf16)
        b_all[h].start()
        return jnp.sum((norm - 1.0) ** 2, axis=0, keepdims=True)

    def weight_terms(dx, h):
        arrived(big, b_send, b_recv, dx, h)
        mine = pl.ds(pl.multiple_of(dp * part, 128), part)
        mixed_part = mixed[h, dx, :, :, :, mine].reshape(lot, part)
        big_part = big[h, dx, :, :, :, mine].reshape(lot, part)
        @tiles(hidden)
        def _(units):
            p = product(w_t[units, :], block(big, dx, h))
            dz = p * d2[dx, h, units, :]
            ph = p * d1[dx, h, units, :]
            lane = lax.broadcasted_iota(jnp.int32, (tile, 128), 1)
            row = sums[units, :]
            row = jnp.where(lane == 2 * dx + h, jnp.sum(dz, axis=1, keepdims=True), row)
            row = jnp.where(lane == 8 + 2 * dx + h, jnp.sum(ph, axis=1, keepdims=True), row)
            sums[units, :] = row
            term = jnp.dot(dz.astype(bf16), mixed_part, preferred_element_type=f32)
            term = term + jnp.dot(u[dx, h, units, :], big_part, preferred_element_type=f32)
            out[units, :] += term

    hops = [dev(0, 0, 1)]
    bit = 1
    while bit < nz:
        hops.append(dev(0, bit, 0))
        bit *= 2
    hops += [dev(1, 0, 0), dev(2, 0, 0)]

    def loss_copy(i):
        return pltpu.make_async_remote_copy(
            src_ref=loss.at[i], dst_ref=loss_in.at[i], send_sem=l_send.at[i],
            recv_sem=l_recv.at[i], device_id=hops[i], device_id_type=MESH,
        )

    def loss_step(i):
        loss_copy(i).wait_recv()
        loss[i + 1] = loss[i] + loss_in[i]
        if i + 1 < len(hops):
            loss_copy(i + 1).start()

    m_all[0].start()
    m_all[1].start()
    for ref, col in ((bias, bias_col), (head, head_col)):
        col[...] = jnp.broadcast_to(ref[...].reshape(1, hidden), (128, hidden)).T
    load_w.wait()
    @tiles(hidden, 256)
    def _(cols):
        w_t[cols, :] = w[:, cols].T
    m_all[0].spread(*others)

    def after_hidden(n):
        if n == 0:
            m_all[0].turn(*every)
        elif n == 1:
            pair_sum(0)
            m_all[1].spread(*others)
        elif n == 2:
            m_all[0].last(*every)
        elif n == 3:
            pair_sum(1)
            loss[0] = jnp.broadcast_to(scale_rows(0), loss.shape[1:])
        elif n == 4:
            b_all[0].spread(1)
            m_all[1].turn(*every)
        elif n == 5:
            b_all[0].spread(*others[1:])
        elif n == 6:
            loss[0] += jnp.broadcast_to(scale_rows(1), loss.shape[1:])
            loss_copy(0).start()
            m_all[1].last(*every)
            b_all[0].turn(*every[:2])
        else:
            loss_step(0)
            b_all[0].turn(*every[2:])
            b_all[1].spread(1)

    order = ((0, 0), (1, 0), (0, 1), (2, 0), (3, 0), (1, 1), (2, 1), (3, 1))

    def hidden_step(n, carry):
        dx, h = n * 0, n * 0
        for i, (group, half) in enumerate(order):
            dx = jnp.where(n == i, group, dx)
            h = jnp.where(n == i, half, h)
        hidden_units(dx, h)

        @pl.when(jnp.logical_or(n == 0, n == 2))
        def _():
            input_gradient(h)

        for i in range(len(order)):
            pl.when(n == i)(functools.partial(after_hidden, i))
        return carry

    lax.fori_loop(0, len(order), hidden_step, 0)

    out[...] = jnp.zeros_like(out)
    sums[...] = jnp.zeros_like(sums)

    def before_weights(n):
        if n == 0:
            b_all[1].spread(*others[1:])
        elif n == 2:
            b_all[0].last(*every)
            b_all[1].turn(*every[:2])
        elif n == 3:
            b_all[1].turn(*every[2:])
        elif n == 5:
            b_all[1].last(*every)
        if n + 1 < len(hops):
            loss_step(n + 1)

    def weight_step(n, carry):
        for i in range(len(order)):
            pl.when(n == i)(functools.partial(before_weights, i))
        weight_terms(lax.rem(n, 4), n // 4)
        return carry

    lax.fori_loop(0, len(order), weight_step, 0)
    for i in range(len(order) + 1, len(hops)):
        loss_step(i)

    by_lot = sums[...].T
    for ref, first in ((out_bias, 0), (out_head, 8)):
        group = [by_lot[first + i:first + i + 1] + by_lot[first + i + 1:first + i + 2] for i in (0, 2, 4, 6)]
        ref[...] = ((group[0] + group[1]) + (group[2] + group[3])).reshape(hidden)
    out_pen[0, 0] = (10.0 * loss[len(hops)] / total_rows)[0, 0]

    for h in range(2):
        m_all[h].finish()
        b_all[h].finish()
        pair_copy(h).wait_send()
        for k in others:
            z_copy(h, k).wait_send()
    for i in range(len(hops)):
        loss_copy(i).wait_send()


def scratch_of(rows, feats, hidden, part, nz):
    f32, bf16 = jnp.float32, jnp.bfloat16
    hops = nz.bit_length() + 2
    lot = nz * rows
    held = [
        ((feats, hidden), bf16),
        ((hidden, feats), bf16),
        ((2, 4, nz, 2, rows // 2, feats), bf16),
        ((2, 4, nz, 2, rows // 2, feats), bf16),
        ((4, 2, hidden, lot), bf16),
        ((4, 2, hidden, lot), f32),
        ((4, 2, hidden, lot), f32),
        ((2, nz, rows // 2, feats), f32),
        ((2, nz, rows // 2, feats), bf16),
        ((2, nz, rows // 2, feats), bf16),
        ((2, nz, rows // 2, feats), bf16),
        ((2, nz, rows // 2, feats), bf16),
        ((hidden, 128), f32),
        ((hops + 1, 8, 128), f32),
        ((hops + 1, 8, 128), f32),
        ((hidden, 128), f32),
        ((hidden, 128), f32),
    ]
    moves = nz - 1 + 8 * nz
    sems = [(), (2, moves), (2, moves), (2, moves), (2, moves), (2,), (2,), (2, nz), (2, nz), (hops,), (hops,)]
    return held, sems


def solution(mesh):
    placed = (
        P(("dp", "tensor"), None),
        P(("dp", "tensor"), None),
        P(("dp", "tensor")),
        P(None, "tensor"),
        P("tensor"),
        P("tensor"),
    )
    groups, members = mesh.shape["dp"], mesh.shape["tensor"]
    nz = members // 2

    def body(real_feats, fake_feats, mix_num, w_first, bias, head):
        rows, feats = real_feats.shape
        hidden = w_first.shape[1]
        part = feats // groups
        held, sems = scratch_of(rows, feats, hidden, part, max(nz, 2))
        size = part * hidden * 4
        for shape, dtype in held:
            size += functools.reduce(lambda a, b: a * b, shape) * jnp.dtype(dtype).itemsize
        tile = next((t for t in (512, 256) if hidden % t == 0 and feats % t == 0), 0)
        fits = (
            groups == 4 and members % 2 == 0 and nz >= 2 and nz & (nz - 1) == 0
            and tile and rows % 64 == 0 and nz * rows % 128 == 0 and part % 128 == 0 and size <= HELD_BYTES
        )
        if not fits:
            return local(real_feats, fake_feats, mix_num, w_first, bias, head)
        vmem = pl.BlockSpec(memory_space=pltpu.VMEM)
        total_rows = rows * groups * members
        grad_w, grad_bias, grad_head, pen = pl.pallas_call(
            functools.partial(kernel, nz, tile, total_rows),
            out_shape=(
                jax.ShapeDtypeStruct((hidden, part), jnp.float32),
                jax.ShapeDtypeStruct((hidden,), jnp.float32),
                jax.ShapeDtypeStruct((hidden,), jnp.float32),
                jax.ShapeDtypeStruct((1, 1), jnp.float32),
            ),
            in_specs=[vmem, vmem, vmem, pl.BlockSpec(memory_space=pl.ANY), vmem, vmem],
            out_specs=(vmem, vmem, vmem, pl.BlockSpec(memory_space=pltpu.SMEM)),
            scratch_shapes=[pltpu.VMEM(s, t) for s, t in held]
            + [pltpu.SemaphoreType.DMA(s) if s else pltpu.SemaphoreType.DMA for s in sems],
            compiler_params=pltpu.CompilerParams(
                collective_id=0, has_side_effects=True, vmem_limit_bytes=VMEM_BYTES
            ),
        )(real_feats, fake_feats, mix_num, w_first, bias, head)
        return (grad_w.T, grad_bias, grad_head, pen.reshape(()))

    return jax.shard_map(
        body,
        mesh=mesh,
        in_specs=placed,
        out_specs=(P("dp", "tensor"), P("tensor"), P("tensor"), P()),
        check_vma=False,
    )
```

```python
import functools

import jax
import jax.numpy as jnp
from jax import lax
from jax.experimental import pallas as pl
from jax.experimental.pallas import tpu as pltpu
from jax.sharding import PartitionSpec as P

MESH = pl.DeviceIdType.MESH
VMEM_BYTES = 62 * 2**20
HELD_BYTES = 58 * 2**20


def row_contract(left, right):
    return lax.dot_general(
        left, right, (((0,), (0,)), ((), ())), preferred_element_type=jnp.float32
    )


def local(real_feats, fake_feats, mix_num, w_first, bias, head):
    coef = mix_num.astype(jnp.float32) / 256.0
    real_f = real_feats.astype(jnp.float32)
    mixed = (real_f + coef[:, None] * (fake_feats.astype(jnp.float32) - real_f)).astype(
        jnp.bfloat16
    )
    group = lax.all_gather(mixed, "tensor", axis=0, tiled=True)
    z = jnp.dot(group, w_first, preferred_element_type=jnp.float32) + bias
    sg = jax.nn.sigmoid(z)
    d1 = sg * (1.0 + z * (1.0 - sg))
    d2 = sg * (1.0 - sg) * (2.0 + z * (1.0 - 2.0 * sg))
    u = (d1 * head).astype(jnp.bfloat16)
    total_rows = group.shape[0] * lax.axis_size("dp")
    grad_in = lax.psum_scatter(
        lax.dot_general(
            u, w_first, (((1,), (1,)), ((), ())), preferred_element_type=jnp.float32
        ).astype(jnp.bfloat16),
        "tensor",
        scatter_dimension=0,
        tiled=True,
    ).astype(jnp.float32)
    norm = jnp.sqrt(jnp.sum(grad_in * grad_in, axis=1) + 1e-06)
    scale = 20.0 * (norm - 1.0) / norm
    scaled = (scale[:, None] * grad_in).astype(jnp.bfloat16)
    loss = lax.psum(jnp.sum((norm - 1.0) ** 2), ("dp", "tensor"))
    big = lax.all_gather(scaled, "tensor", axis=0, tiled=True)
    penalty = 10.0 * loss / total_rows
    p = jnp.dot(big, w_first, preferred_element_type=jnp.float32)
    dz = p * head * d2
    dzb = dz.astype(jnp.bfloat16)
    partial_w = row_contract(group, dzb)
    partial_w = partial_w + row_contract(big, u)
    grad_w = lax.psum_scatter(partial_w, "dp", scatter_dimension=0, tiled=True)
    grad_bias, grad_head = lax.psum((jnp.sum(dz, axis=0), jnp.sum(p * d1, axis=0)), "dp")
    return (grad_w, grad_bias, grad_head, penalty)


def flip(index, mask):
    bit = 1
    while bit <= mask:
        if mask & bit:
            index = index + bit - 2 * bit * lax.rem(index // bit, 2)
        bit *= 2
    return index


def relays(nz):
    return {2: (3, 1)} if nz == 4 else {}


class Gather:
    def __init__(self, held, nz, send, recv, dev):
        self.held, self.nz, self.dev = held, nz, dev
        self.send, self.recv = send, recv
        self.via = relays(nz)
        self.names = (
            [("z", 0, k) for k in range(1, nz)]
            + [(kind, dx, k) for kind, dxs in (("c", range(4)), ("xy", (1, 2)), ("d", (0, 1)))
               for dx in dxs for k in range(nz)]
        )

    def copy(self, name):
        kind, dx, k = name
        held, dev = self.held, self.dev
        half = held.shape[3] // 2
        if kind == "z" and k in self.via:
            held_at, step = self.via[k]
            src, dst, to = held.at[0, held_at, 0], held.at[0, k, 0], dev(0, step, 0)
        elif kind == "z":
            src, dst, to = held.at[0, 0, 0], held.at[0, k, 0], dev(0, k, 0)
        elif kind == "c":
            src, dst, to = held.at[dx, k, 0], held.at[dx, k, 1], dev(0, 0, 1)
        elif kind == "xy":
            src, dst, to = held.at[0, k, 0], held.at[dx, k, 0], dev(dx, 0, 0)
        else:
            rows = pl.ds(dx * half, half)
            src, dst, to = held.at[1 + dx, k, 0, rows], held.at[3, k, 0, rows], dev(2 - dx, 0, 0)
        i = self.names.index(name)
        return pltpu.make_async_remote_copy(
            src_ref=src, dst_ref=dst, send_sem=self.send.at[i], recv_sem=self.recv.at[i],
            device_id=to, device_id_type=MESH,
        )

    def start(self):
        for k in range(1, self.nz):
            if k not in self.via:
                self.copy(("z", 0, k)).start()
        self.spread(0)

    def spread(self, *ks):
        for k in ks:
            if k:
                self.copy(("z", 0, k)).wait_recv()
            for later, (held_at, _) in self.via.items():
                if held_at == k:
                    self.copy(("z", 0, later)).start()
            for name in (("xy", 1, k), ("xy", 2, k), ("c", 0, k)):
                self.copy(name).start()

    def turn(self, *ks):
        for k in ks:
            for dx in (1, 2):
                self.copy(("xy", dx, k)).wait_recv()
                self.copy(("d", dx - 1, k)).start()
                self.copy(("c", dx, k)).start()

    def last(self, *ks):
        for k in ks:
            self.copy(("d", 0, k)).wait_recv()
            self.copy(("d", 1, k)).wait_recv()
            self.copy(("c", 3, k)).start()

    def arrived(self, dx):
        for k in range(self.nz):
            self.copy(("c", dx, k)).wait_recv()

    def finish(self):
        for name in self.names:
            self.copy(name).wait_send()


def kernel(
    nz, tile, total_rows,
    real, fake, mix, w_hbm, bias, head,
    out, out_bias, out_head, out_pen,
    w, mixed, big, u, d1, d2, own, lhs, to_pair, from_pair, to_z, from_z,
    sum_bias, sum_head, loss, loss_in, bias_row, head_row,
    w_sem, m_send, m_recv, b_send, b_recv, p_send, p_recv, z_send, z_recv, l_send, l_recv,
):
    f32, bf16 = jnp.float32, jnp.bfloat16
    dp, tensor = lax.axis_index("dp"), lax.axis_index("tensor")
    z_at, core = tensor // 2, lax.rem(tensor, 2)
    feats = real.shape[1]
    rows = real.shape[0] // 2
    lot = 2 * nz * rows
    hidden = w.shape[1]
    part = out.shape[0]
    via = relays(nz)
    every = tuple(range(nz))
    others = tuple(k for k in every[1:] if k not in via) + tuple(via)

    def dev(dx, zx, cc):
        return (flip(dp, dx), flip(z_at, zx) * 2 + flip(core, cc))

    load_w = pltpu.make_async_copy(w_hbm, w, w_sem)
    load_w.start()
    partners = [dev(0, 0, 1), dev(1, 0, 0), dev(2, 0, 0)]
    partners += [dev(0, k, 0) for k in others]
    barrier = pltpu.get_barrier_semaphore()
    for to in partners:
        pl.semaphore_signal(barrier, inc=1, device_id=to, device_id_type=MESH)
    count = mix.shape[0]
    places = [lax.broadcasted_iota(jnp.int32, (count, count), axis) for axis in (0, 1)]
    spread = jnp.broadcast_to(mix[...].reshape(1, count).astype(f32), (count, count))
    spread = jnp.where(places[0] == places[1], spread, 0.0)
    coef = jnp.sum(spread, axis=1, keepdims=True) / 256.0
    real_f = real[...].astype(f32)
    rows_in = (real_f + coef * (fake[...].astype(f32) - real_f)).astype(bf16)
    for h in range(2):
        mixed[h, 0, 0, 0] = rows_in[h * rows:(h + 1) * rows]
    bias_row[...] = bias[...].reshape(1, hidden)
    head_row[...] = head[...].reshape(1, hidden)
    pl.semaphore_wait(barrier, len(partners))

    m_all = [Gather(mixed.at[h], nz, m_send.at[h], m_recv.at[h], dev) for h in range(2)]
    b_all = [Gather(big.at[h], nz, b_send.at[h], b_recv.at[h], dev) for h in range(2)]

    def block(held, dx, h):
        return held[h, dx].reshape(lot, feats)

    def columns(i):
        return pl.ds(pl.multiple_of(i * tile, tile), tile)

    def hidden_units(dx, h):
        m_all[h].arrived(dx)

        def step(i, carry):
            cols = columns(i)
            z = jnp.dot(block(mixed, dx, h), w[:, cols], preferred_element_type=f32)
            z = z + bias_row[:, cols]
            t = jnp.tanh(0.5 * z)
            sg = 0.5 + 0.5 * t
            slope = 0.25 * (1.0 - t * t)
            first = sg + z * slope
            second = slope * (2.0 - z * t)
            by = head_row[:, cols]
            d1[dx, h, :, cols] = first
            d2[dx, h, :, cols] = second * by
            u[dx, h, :, cols] = (first * by).astype(bf16)
            return carry

        lax.fori_loop(0, hidden // tile, step, 0)

    def pair_copy(h):
        return pltpu.make_async_remote_copy(
            src_ref=to_pair.at[h], dst_ref=from_pair.at[h], send_sem=p_send.at[h],
            recv_sem=p_recv.at[h], device_id=dev(0, 0, 1), device_id_type=MESH,
        )

    def z_copy(h, k):
        return pltpu.make_async_remote_copy(
            src_ref=to_z.at[h, k], dst_ref=from_z.at[h, k], send_sem=z_send.at[h, k],
            recv_sem=z_recv.at[h, k], device_id=dev(0, via[k][1] if k in via else k, 0),
            device_id_type=MESH,
        )

    def input_gradient(h):
        def step(i, carry):
            cols = columns(i)
            g = lax.dot_general(
                u[0, h], w[cols, :], (((1,), (1,)), ((), ())), preferred_element_type=f32
            ).reshape(nz, 2, rows, tile)
            for k in every:
                own[h, k, :, cols] = g[k, 0]
                to_pair[h, k, :, cols] = g[k, 1].astype(bf16)
            return carry

        lax.fori_loop(0, feats // tile, step, 0)
        pair_copy(h).start()

    merged = {held_at: k for k, (held_at, _) in via.items()}

    def pair_sum(h):
        pair_copy(h).wait_recv()
        for k in tuple(via) + tuple(k for k in every if k not in via):
            both = own[h, k] + from_pair[h, k].astype(f32)
            if k in merged or k == 0:
                own[h, k] = both
            else:
                to_z[h, k] = both.astype(bf16)
                z_copy(h, k).start()

    def relay_sum(h):
        for k, passed in merged.items():
            z_copy(h, passed).wait_recv()
            to_z[h, k] = (own[h, k] + from_z[h, passed].astype(f32)).astype(bf16)
            z_copy(h, k).start()

    def scale_rows(h):
        g = own[h, 0]
        for k in others:
            if k not in via:
                z_copy(h, k).wait_recv()
                g = g + from_z[h, k].astype(f32)
        norm = jnp.sqrt(jnp.sum(g * g, axis=1, keepdims=True) + 1e-06)
        big[h, 0, 0, 0] = (20.0 * (norm - 1.0) / norm * g).astype(bf16)
        b_all[h].start()
        return jnp.sum((norm - 1.0) ** 2, axis=0, keepdims=True)

    def weight_terms(dx, h, start=False):
        b_all[h].arrived(dx)
        mine = pl.ds(pl.multiple_of(dp * part, 128), part)
        for j, held in enumerate((mixed, big)):
            lhs[j] = held[h, dx, :, :, :, mine].reshape(lot, part).T

        def step(i, carry):
            cols = columns(i)
            p = jnp.dot(block(big, dx, h), w[:, cols], preferred_element_type=f32)
            dz = p * d2[dx, h, :, cols]
            ph = p * d1[dx, h, :, cols]
            add_bias = jnp.sum(dz.reshape(lot // 8, 8, tile), axis=0)
            add_head = jnp.sum(ph.reshape(lot // 8, 8, tile), axis=0)
            if h == 0:
                sum_bias[dx, :, cols] = add_bias
                sum_head[dx, :, cols] = add_head
            else:
                sum_bias[dx, :, cols] += add_bias
                sum_head[dx, :, cols] += add_head
            term = jnp.dot(lhs[0], dz.astype(bf16), preferred_element_type=f32)
            term = term + jnp.dot(lhs[1], u[dx, h, :, cols], preferred_element_type=f32)
            if start:
                out[:, cols] = term
            else:
                out[:, cols] += term
            return carry

        lax.fori_loop(0, hidden // tile, step, 0)

    hops = [dev(0, 0, 1)]
    bit = 1
    while bit < nz:
        hops.append(dev(0, bit, 0))
        bit *= 2
    hops += [dev(1, 0, 0), dev(2, 0, 0)]

    def loss_copy(i):
        return pltpu.make_async_remote_copy(
            src_ref=loss.at[i], dst_ref=loss_in.at[i], send_sem=l_send.at[i],
            recv_sem=l_recv.at[i], device_id=hops[i], device_id_type=MESH,
        )

    state = [0]

    def loss_step():
        i = state[0]
        if i < len(hops):
            loss_copy(i).wait_recv()
            loss[i + 1] = loss[i] + loss_in[i]
            if i + 1 < len(hops):
                loss_copy(i + 1).start()
            state[0] = i + 1

    m_all[0].start()
    m_all[1].start()
    load_w.wait()
    m_all[0].spread(*others)
    hidden_units(0, 0)
    input_gradient(0)
    m_all[0].turn(*every)
    hidden_units(1, 0)
    pair_sum(0)
    m_all[1].spread(others[0])
    relay_sum(0)
    m_all[1].spread(*others[1:])
    hidden_units(0, 1)
    input_gradient(1)
    m_all[0].last(*every)
    hidden_units(2, 0)
    pair_sum(1)
    miss = scale_rows(0)
    relay_sum(1)
    hidden_units(3, 0)
    b_all[0].spread(others[0])
    m_all[1].turn(*every)
    hidden_units(1, 1)
    b_all[0].spread(*others[1:])
    hidden_units(2, 1)
    miss = miss + scale_rows(1)
    loss[0] = jnp.broadcast_to(miss, loss.shape[1:])
    loss_copy(0).start()
    m_all[1].last(*every)
    b_all[0].turn(0, 1)
    hidden_units(3, 1)
    loss_step()

    b_all[0].turn(*every[2:])
    b_all[1].spread(others[0])
    weight_terms(0, 0, True)
    loss_step()
    b_all[1].spread(*others[1:])
    weight_terms(1, 0)
    loss_step()
    b_all[0].last(*every)
    b_all[1].turn(0, 1)
    weight_terms(2, 0)
    loss_step()
    b_all[1].turn(*every[2:])
    weight_terms(3, 0)
    loss_step()
    weight_terms(0, 1)
    b_all[1].last(*every)
    weight_terms(1, 1)
    weight_terms(2, 1)
    weight_terms(3, 1)
    while state[0] < len(hops):
        loss_step()

    for ref, sums in ((out_bias, sum_bias), (out_head, sum_head)):
        whole = (sums[0] + sums[1]) + (sums[2] + sums[3])
        ref[...] = jnp.sum(whole, axis=0, keepdims=True).reshape(hidden)
    out_pen[0, 0] = (10.0 * loss[len(hops)] / total_rows)[0, 0]

    for h in range(2):
        m_all[h].finish()
        b_all[h].finish()
        pair_copy(h).wait_send()
        for k in others:
            z_copy(h, k).wait_send()
    for i in range(len(hops)):
        loss_copy(i).wait_send()


def scratch_of(rows, feats, hidden, part, nz):
    f32, bf16 = jnp.float32, jnp.bfloat16
    hops = nz.bit_length() + 2
    lot = nz * rows
    held = [
        ((feats, hidden), bf16),
        ((2, 4, nz, 2, rows // 2, feats), bf16),
        ((2, 4, nz, 2, rows // 2, feats), bf16),
        ((4, 2, lot, hidden), bf16),
        ((4, 2, lot, hidden), f32),
        ((4, 2, lot, hidden), f32),
        ((2, nz, rows // 2, feats), f32),
        ((2, part, lot), bf16),
        ((2, nz, rows // 2, feats), bf16),
        ((2, nz, rows // 2, feats), bf16),
        ((2, nz, rows // 2, feats), bf16),
        ((2, nz, rows // 2, feats), bf16),
        ((4, 8, hidden), f32),
        ((4, 8, hidden), f32),
        ((hops + 1, 8, 128), f32),
        ((hops + 1, 8, 128), f32),
        ((1, hidden), f32),
        ((1, hidden), f32),
    ]
    moves = nz - 1 + 8 * nz
    sems = [(), (2, moves), (2, moves), (2, moves), (2, moves), (2,), (2,), (2, nz), (2, nz), (hops,), (hops,)]
    return held, sems


def solution(mesh):
    placed = (
        P(("dp", "tensor"), None),
        P(("dp", "tensor"), None),
        P(("dp", "tensor")),
        P(None, "tensor"),
        P("tensor"),
        P("tensor"),
    )
    groups, members = mesh.shape["dp"], mesh.shape["tensor"]
    nz = members // 2

    def body(real_feats, fake_feats, mix_num, w_first, bias, head):
        rows, feats = real_feats.shape
        hidden = w_first.shape[1]
        part = feats // groups
        held, sems = scratch_of(rows, feats, hidden, part, max(nz, 2))
        size = part * hidden * 4
        for shape, dtype in held:
            size += functools.reduce(lambda a, b: a * b, shape) * jnp.dtype(dtype).itemsize
        tile = next((t for t in (512, 256, 128) if hidden % t == 0 and feats % t == 0), 0)
        fits = (
            groups == 4 and members % 2 == 0 and nz >= 2 and nz & (nz - 1) == 0
            and tile and rows % 64 == 0 and part % 128 == 0 and size <= HELD_BYTES
        )
        if not fits:
            return local(real_feats, fake_feats, mix_num, w_first, bias, head)
        vmem = pl.BlockSpec(memory_space=pltpu.VMEM)
        total_rows = rows * groups * members
        grad_w, grad_bias, grad_head, pen = pl.pallas_call(
            functools.partial(kernel, nz, tile, total_rows),
            out_shape=(
                jax.ShapeDtypeStruct((part, hidden), jnp.float32),
                jax.ShapeDtypeStruct((hidden,), jnp.float32),
                jax.ShapeDtypeStruct((hidden,), jnp.float32),
                jax.ShapeDtypeStruct((1, 1), jnp.float32),
            ),
            in_specs=[vmem, vmem, vmem, pl.BlockSpec(memory_space=pl.ANY), vmem, vmem],
            out_specs=(vmem, vmem, vmem, pl.BlockSpec(memory_space=pltpu.SMEM)),
            scratch_shapes=[pltpu.VMEM(s, t) for s, t in held]
            + [pltpu.SemaphoreType.DMA(s) if s else pltpu.SemaphoreType.DMA for s in sems],
            compiler_params=pltpu.CompilerParams(
                collective_id=0, has_side_effects=True, vmem_limit_bytes=VMEM_BYTES
            ),
        )(real_feats, fake_feats, mix_num, w_first, bias, head)
        return (grad_w, grad_bias, grad_head, pen.reshape(()))

    return jax.shard_map(
        body,
        mesh=mesh,
        in_specs=placed,
        out_specs=(P("dp", "tensor"), P("tensor"), P("tensor"), P()),
        check_vma=False,
    )
```
